128 devices in a mesh: gz: 64 (over x, y, z), gy: 2 (over core).
Axes of the slice: x: 4, y: 4, z: 4, core: 2. Of those that a mesh axis runs over, the one named last changes fastest.
Arguments:
- observed: float32 [512, 128, 512], P('gz', 'gy'), may hold values from 0.28 to 10.5, as said below
- psf_taps: float32 [8, 3, 15], replicated, may hold values from 0.05 to 1
- psf_index: int32 [512], replicated, may hold values from 0 to 7
- tissue: int32 [64, 4, 16], P('gz', 'gy'), may hold values from 0 to 1, as said below
- w_first: bfloat16 [32, 27], replicated, may hold values from -1.25 to 1.25
- b_first: float32 [32], replicated, may hold values from -3 to 3
- w_mid: bfloat16 [27, 32, 32], replicated, may hold values from -0.21875 to 0.21875
- b_mid: float32 [32], replicated, may hold values from -3 to 3
- w_last: bfloat16 [32], replicated, may hold values from -1 to 1
- b_last: float32 [1], replicated, may hold values from -2 to 2
Outputs:
- restored: float32 [512, 128, 512], P('gz', 'gy')
The draws below stay inside these ranges and needn't reach their ends.
Inputs may be any that keep to these rules, and one draw needn't show every extreme that they name: `observed`: recorded intensities are positive. The 2 by 16 bricks of one device hold at most 3 tissue bricks, and some device holds exactly 3. Number the devices by slab times 2 plus row strip; every aligned group of 4 devices (two neighbouring slabs, both strips) holds exactly 4 tissue bricks.
All inputs are finite; a program needn't handle non-finite values.
Results may differ from the reference program's by a relative error of at most 0.0018.
Values may be sent and summed in bfloat16 or wider, within the bound.
No kernel may reach another device: no remote copies, remote signals or barrier semaphores. Data moves between devices by JAX's collectives and lax.ppermute only.
A program may use at most 128 MiB of HBM per device.

```python
import math
import jax
import jax.numpy as jnp
from jax import lax

SZ = 8
SY = 64
NX = 512
MEANT = 1
BY = 32
BX = 32
TAPS = 15
KPSF = 8
ROUNDS = 2
CH = 32
NZ = 512
NY = 128
N_GZ = 64
N_GY = 2


def draw_observed(key, part):
    key = jax.random.fold_in(key, 11)
    depth_share = jnp.arange(NZ, dtype=jnp.float32) / (NZ - 1)
    attenuation = (1.0 + 2.0 * depth_share)[:, None, None]
    texture = jnp.exp(0.5 * jnp.clip(jax.random.normal(key, (NZ, NY, NX), jnp.float32), -2.5, 2.5))
    return attenuation * texture


def draw_tissue(key, part):
    key = jax.random.fold_in(key, 23)
    slab_count = NZ // SZ
    strip_count = NY // SY
    devices = slab_count * strip_count
    groups = devices // 4
    heavy_key = jax.random.fold_in(key, 1)
    choose_key = jax.random.fold_in(key, 2)
    light_key = jax.random.fold_in(key, 3)
    shuffle_key = jax.random.fold_in(key, 4)
    ranking_key = jax.random.fold_in(key, 5)
    heavy_cut = jax.random.randint(heavy_key, (groups,), 0, 3 * MEANT + 1)
    chosen = jax.random.randint(choose_key, (), 0, groups)
    heavy_cut = jnp.where(jnp.arange(groups, dtype=jnp.int32) == chosen, 0, heavy_cut)
    light_cut = jax.random.randint(light_key, (groups,), 0, MEANT + 1)
    shares = jnp.stack([3 * MEANT - heavy_cut, heavy_cut, light_cut, MEANT - light_cut], axis=1)
    shuffle = jax.vmap(lambda sub_key: jax.random.permutation(sub_key, 4))(jax.random.split(shuffle_key, groups))
    counts = jnp.take_along_axis(shares, shuffle, axis=1).reshape(devices)
    bricks_down = SY // BY
    bricks_across = NX // BX
    ranking = jax.vmap(lambda sub_key: jax.random.permutation(sub_key, bricks_down * bricks_across))(jax.random.split(ranking_key, devices))
    marked = (ranking < counts[:, None]).astype(jnp.int32)
    return marked.reshape(slab_count, strip_count * bricks_down, bricks_across)


def with_ends(drawn, own_key, least, largest):
    shape = drawn.shape
    place = [jax.random.randint(jax.random.fold_in(own_key, axis), (), 0, shape[axis]) for axis in range(len(shape))]
    drawn = drawn.at[tuple(place)].set(least)
    longest = shape.index(max(shape))
    place[longest] = (place[longest] + 1) % shape[longest]
    return drawn.at[tuple(place)].set(largest)


def gaussian(stream_key, shape, width, reach, held_as=jnp.bfloat16):
    return jnp.clip(width * jax.random.normal(stream_key, shape, jnp.float32), -reach, reach).astype(held_as)


def setup_inputs(seed: int = 0) -> dict:
    splits = jax.random.split(jax.random.key(seed), 11)
    observed = draw_observed(jax.random.fold_in(splits[10], 71), 0)
    psf_taps = jnp.clip(jnp.exp(jax.random.uniform(splits[1], (KPSF, 3, TAPS), jnp.float32, math.log(0.05), math.log(1.0))), 0.05, 1.0)
    psf_index = with_ends(jax.random.randint(splits[2], (NZ,), 0, KPSF), jax.random.fold_in(splits[2], 1), 0, KPSF - 1).astype(jnp.int32)
    tissue = draw_tissue(jax.random.fold_in(splits[10], 71), 0)
    w_first = gaussian(splits[4], (CH, 27), 27 ** -0.5, 1.25)
    b_first = gaussian(splits[5], (CH,), 0.5, 3.0, jnp.float32)
    w_mid = gaussian(splits[6], (27, CH, CH), (27 * CH) ** -0.5, 0.21875)
    b_mid = gaussian(splits[7], (CH,), 0.5, 3.0, jnp.float32)
    w_last = gaussian(splits[8], (CH,), CH ** -0.5, 1.0)
    b_last = gaussian(splits[9], (1,), 0.3, 2.0, jnp.float32)
    return dict(observed=observed, psf_taps=psf_taps, psf_index=psf_index, tissue=tissue, w_first=w_first, b_first=b_first, w_mid=w_mid, b_mid=b_mid, w_last=w_last, b_last=b_last)


def plane_kernels(psf_taps, psf_index):
    normed_taps = psf_taps / lax.optimization_barrier(jnp.sum(psf_taps, axis=2, keepdims=True))
    models = jnp.arange(psf_taps.shape[0], dtype=jnp.int32)
    picker = (psf_index[:, None] == models[None, :]).astype(jnp.float32)
    return jnp.einsum('zk,kat->zat', picker, normed_taps, precision=lax.Precision.HIGHEST)

def forward_blur(padded, kernels):
    tap_count = kernels.shape[2]
    margin = tap_count // 2
    plane_count = padded.shape[0] - 2 * margin
    row_count = padded.shape[1] - 2 * margin
    column_count = padded.shape[2]
    own_kernels = kernels[margin:margin + plane_count]
    depth_pass = jnp.zeros((plane_count, padded.shape[1], column_count), jnp.float32)
    for tap_index in range(tap_count):
        depth_pass = depth_pass + own_kernels[:, 0, tap_index][:, None, None] * padded[tap_index:tap_index + plane_count]
    row_pass = jnp.zeros((plane_count, row_count, column_count), jnp.float32)
    for tap_index in range(tap_count):
        row_pass = row_pass + own_kernels[:, 1, tap_index][:, None, None] * depth_pass[:, tap_index:tap_index + row_count]
    widened = jnp.pad(row_pass, ((0, 0), (0, 0), (margin, margin)))
    result = jnp.zeros((plane_count, row_count, column_count), jnp.float32)
    for tap_index in range(tap_count):
        result = result + own_kernels[:, 2, tap_index][:, None, None] * widened[:, :, tap_index:tap_index + column_count]
    return result

def adjoint_blur(padded, kernels):
    tap_count = kernels.shape[2]
    margin = tap_count // 2
    plane_count = padded.shape[0] - 2 * margin
    row_count = padded.shape[1] - 2 * margin
    column_count = padded.shape[2]
    widened = jnp.pad(padded, ((0, 0), (0, 0), (margin, margin)))
    across = jnp.zeros(padded.shape, jnp.float32)
    for tap_index in range(tap_count):
        start = 2 * margin - tap_index
        across = across + kernels[:, 2, tap_index][:, None, None] * widened[:, :, start:start + column_count]
    along = jnp.zeros((padded.shape[0], row_count, column_count), jnp.float32)
    for tap_index in range(tap_count):
        start = 2 * margin - tap_index
        along = along + kernels[:, 1, tap_index][:, None, None] * across[:, start:start + row_count]
    result = jnp.zeros((plane_count, row_count, column_count), jnp.float32)
    for tap_index in range(tap_count):
        start = 2 * margin - tap_index
        result = result + kernels[start:start + plane_count, 0, tap_index][:, None, None] * along[start:start + plane_count]
    return result

def neighbour_shifts(brick_planes, brick_rows, brick_columns):
    voxel_index = jnp.arange(brick_planes * brick_rows * brick_columns, dtype=jnp.int32)
    plane_at = voxel_index // (brick_rows * brick_columns)
    row_at = voxel_index // brick_columns % brick_rows
    column_at = voxel_index % brick_columns
    shifts = []
    for step_plane in (-1, 0, 1):
        for step_row in (-1, 0, 1):
            for step_column in (-1, 0, 1):
                inside = (plane_at + step_plane >= 0) & (plane_at + step_plane < brick_planes) & (row_at + step_row >= 0) & (row_at + step_row < brick_rows) & (column_at + step_column >= 0) & (column_at + step_column < brick_columns)
                offset = step_plane * brick_rows * brick_columns + step_row * brick_columns + step_column
                shifts.append((offset, inside))
    return shifts

def shifted(values, offset, inside, margin):
    voxels = values.shape[-1]
    padding = [(0, 0)] * (values.ndim - 1) + [(margin, margin)]
    widened = jnp.pad(values, padding)
    moved_values = lax.slice_in_dim(widened, margin + offset, margin + offset + voxels, axis=values.ndim - 1)
    return moved_values * inside.astype(values.dtype)

def restore_net(inputs, w_first, b_first, w_mid, b_mid, w_last, b_last, shifts, margin):
    stacked = jnp.stack([shifted(inputs, offset, inside, margin) for offset, inside in shifts], axis=1).astype(jnp.float32)
    first = jnp.einsum('ot,stv->sov', w_first.astype(jnp.float32), stacked) + b_first[None, :, None]
    hidden_one = jax.nn.relu(first).astype(jnp.bfloat16)
    total = jnp.zeros(first.shape, jnp.float32)
    for tap_index, (offset, inside) in enumerate(shifts):
        moved_hidden = shifted(hidden_one, offset, inside, margin).astype(jnp.float32)
        total = total + jnp.einsum('oc,scv->sov', w_mid[tap_index].astype(jnp.float32), moved_hidden)
    hidden_two = jax.nn.relu(total + b_mid[None, :, None]).astype(jnp.bfloat16)
    return jnp.einsum('c,scv->sv', w_last.astype(jnp.float32), hidden_two.astype(jnp.float32)) + b_last[0]

def reference(observed, psf_taps, psf_index, tissue, w_first, b_first, w_mid, b_mid, w_last, b_last):
    kernels = plane_kernels(psf_taps, psf_index)
    margin = psf_taps.shape[2] // 2
    extended = jnp.pad(kernels, ((margin, margin), (0, 0), (0, 0)))

    def surround(volume):
        return jnp.pad(volume, ((margin, margin), (margin, margin), (0, 0)))
    normalizer = adjoint_blur(surround(jnp.ones_like(observed)), extended)
    estimate = observed
    for round_index in range(ROUNDS):
        blurred = forward_blur(surround(estimate), extended)
        estimate = estimate * adjoint_blur(surround(observed / blurred), extended) / normalizer
    voxel_total = float(NZ * NY * NX)
    centre = jnp.sum(estimate) / voxel_total
    spread = jnp.sqrt(jnp.sum((estimate - centre) ** 2) / voxel_total + 1e-06)
    normed = ((estimate - centre) / spread).astype(jnp.bfloat16)
    slab_count = NZ // SZ
    voxels = SZ * BY * BX

    def to_bricks(volume):
        blocks = volume.reshape(slab_count, SZ, NY // BY, BY, NX // BX, BX)
        return blocks.transpose(0, 2, 4, 1, 3, 5).reshape(-1, voxels)
    estimate_bricks = to_bricks(estimate)
    normed_bricks = to_bricks(normed)
    tissue_flat = tissue.reshape(-1)
    chosen = jnp.nonzero(tissue_flat, size=MEANT * N_GZ * N_GY, fill_value=0)[0].astype(jnp.int32)
    shifts = neighbour_shifts(SZ, BY, BX)
    margin_voxels = BY * BX + BX + 1

    def one_block(indices):
        return restore_net(normed_bricks[indices], w_first, b_first, w_mid, b_mid, w_last, b_last, shifts, margin_voxels)
    residuals = lax.map(one_block, chosen.reshape(N_GZ * N_GY, MEANT))
    residual_all = jnp.zeros(estimate_bricks.shape, jnp.float32).at[chosen].set(residuals.reshape(-1, voxels))
    restored_bricks = estimate_bricks + spread * residual_all
    blocks = restored_bricks.reshape(slab_count, NY // BY, NX // BX, SZ, BY, BX)
    return blocks.transpose(0, 3, 1, 4, 2, 5).reshape(NZ, NY, NX)
```

```python
import jax
import jax.numpy as jnp
from jax import lax
from jax.experimental import pallas as pl
from jax.experimental.pallas import tpu as pltpu
from jax.sharding import PartitionSpec as P

F32 = jnp.float32
BF16 = jnp.bfloat16
SZ, SY, NX = 8, 64, 512
NZ, NY = 512, 128
TAPS, R = 15, 7
HALO = 16
EXT = SY + HALO
MODELS = 8
BY, BX = 32, 32
CH = 32
SPAN = SZ + 2 * R
COUNT = float(NZ * NY * NX)
LOCAL = float(SZ * SY * NX)
DEVICES = 128
AT_FORWARD = 0
AT_ADJOINT = SZ * SPAN
AT_ROWS = 2 * SZ * SPAN
AT_COLUMNS = AT_ROWS + SZ * TAPS
MIB = 1024 * 1024

VMEM = pl.BlockSpec(memory_space=pltpu.VMEM)
SMEM = pl.BlockSpec(memory_space=pltpu.SMEM)


def iota(shape, axis):
    return lax.broadcasted_iota(jnp.int32, shape, axis)


def call(kernel, outs, ins, specs, scratch=(), flops=0, limit=24):
    moved = sum(x.size * x.dtype.itemsize for x in list(ins) + list(outs))
    return pl.pallas_call(
        kernel,
        out_shape=outs,
        in_specs=specs,
        out_specs=[VMEM] * len(outs),
        scratch_shapes=scratch,
        compiler_params=pltpu.CompilerParams(vmem_limit_bytes=limit * MIB),
        cost_estimate=pl.CostEstimate(flops=flops, bytes_accessed=moved, transcendentals=0),
    )(*ins)


def shape(dims, dtype):
    return jax.ShapeDtypeStruct(dims, dtype)


def send_planes(volume_ref, first_ref, second_ref):
    even = 1 - lax.axis_index("gz") % 2

    @pl.loop(0, R)
    def _(k):
        first_ref[k] = volume_ref[k + even].astype(BF16)
        second_ref[k] = volume_ref[k + 1 - even].astype(BF16)


def edge_rows(volume, rows, gy):
    start = pl.multiple_of((1 - gy) * (SY - rows), rows)
    return volume[:, pl.ds(start, rows), :]


def prepare_kernel(observed_ref, first_ref, second_ref, edge_ref):
    gy = lax.axis_index("gy")
    send_planes(observed_ref, first_ref, second_ref)
    edge_ref[...] = edge_rows(observed_ref, HALO, gy)


def split(value):
    high = value.astype(BF16)
    return high, (value - high.astype(F32)).astype(BF16)


def setup_kernel(
    table_ref, kx_ref, kyt_ref, weight_ref, rows_f_ref, rows_a_ref, cols_f_ref, cols_a_ref, inverse_ref
):
    gy = lax.axis_index("gy")

    def place(index):
        return jnp.where(index < SY, index, jnp.where(gy == 0, index, index - EXT))

    lane = iota((EXT, 256), 1)
    piece = lane // EXT
    inside = place(lane - piece * EXT)
    outside = place(iota((EXT, 256), 0))
    used = piece < 3
    tap_f = jnp.where(used, inside - outside + R, -1)
    tap_a = jnp.where(used, outside - inside + R, -1)[:SY]
    low = piece == 1
    source = iota((256, 128), 0)
    target = iota((256, 128), 1)
    tap_cf = source - target - (64 - R)
    tap_ca = target - source + (64 + R)

    @pl.loop(0, SZ)
    def _(z):
        def table(taps, at):
            total = jnp.zeros(taps.shape, F32)
            for t in range(TAPS):
                total = jnp.where(taps == t, table_ref[at + z * TAPS + t], total)
            return total

        def halves(value, is_low):
            high = value.astype(BF16).astype(F32)
            return jnp.where(is_low, value - high, high).astype(BF16)

        rows_f_ref[z] = halves(table(tap_f, AT_ROWS), low)
        rows_a_ref[z] = halves(table(tap_a, AT_ROWS), low[:SY])
        for taps, out in ((tap_cf, cols_f_ref), (tap_ca, cols_a_ref)):
            high, rest = split(table(taps, AT_COLUMNS))
            out[z, :, :128] = high
            out[z, :, 128:] = rest

    column = iota((1, NX), 1)
    row = iota((SY, 1), 0) + gy * SY
    across = jnp.zeros((24, NX), F32)
    along = jnp.zeros((SY, 128), F32)
    for t in range(TAPS):
        at_x = column + R - t
        at_y = row + R - t
        across += jnp.where((at_x >= 0) & (at_x < NX), kx_ref[:, t : t + 1], 0.0)
        along += jnp.where((at_y >= 0) & (at_y < NY), kyt_ref[t : t + 1, :], 0.0)
    across = jnp.concatenate([across, jnp.zeros((104, NX), F32)], axis=0)
    for z in range(SZ):
        norm = jnp.dot(
            along * weight_ref[z : z + 1, :],
            across,
            precision=lax.Precision.HIGHEST,
            preferred_element_type=F32,
        )
        inverse_ref[z] = 1.0 / norm


def plane_pass(coefficient, own_ref, first_ref, second_ref, emit):
    even = lax.axis_index("gz") % 2 == 0
    high, wide = 16, 256

    def run(low_ref, high_ref):
        @pl.loop(0, SY // high)
        def _(block):
            rows = pl.ds(pl.multiple_of(block * high, high), high)
            for part in range(NX // wide):
                lanes = pl.ds(part * wide, wide)
                planes = [low_ref[k, rows, lanes].astype(F32) for k in range(R)]
                planes += [own_ref[k, rows, lanes] for k in range(SZ)]
                planes += [high_ref[k, rows, lanes].astype(F32) for k in range(R)]
                for z in range(SZ):
                    terms = [coefficient(z, j) * planes[j] for j in range(z, z + TAPS)]
                    while len(terms) > 1:
                        terms = [sum(terms[i : i + 2]) for i in range(0, len(terms), 2)]
                    emit(z, rows, lanes, terms[0])

    @pl.when(even)
    def _():
        run(second_ref, first_ref)

    @pl.when(jnp.logical_not(even))
    def _():
        run(first_ref, second_ref)


def forward_planes_kernel(table_ref, own_ref, first_ref, second_ref, out_ref, edge_ref):
    def emit(z, rows, lanes, value):
        out_ref[z, rows, lanes] = value

    plane_pass(
        lambda z, j: table_ref[AT_FORWARD + z * SPAN + j], own_ref, first_ref, second_ref, emit
    )
    edge_ref[...] = edge_rows(out_ref, HALO, lax.axis_index("gy")).astype(BF16)


def adjoint_coefficient(table_ref):
    return lambda z, j: table_ref[AT_ADJOINT + j * SZ + z]


def update_kernel(
    table_ref, own_ref, first_ref, second_ref, before_ref, inverse_ref, out_ref, to_first_ref, to_second_ref
):
    def emit(z, rows, lanes, value):
        out_ref[z, rows, lanes] = (
            before_ref[z, rows, lanes] * value * inverse_ref[z, rows, lanes]
        )

    plane_pass(adjoint_coefficient(table_ref), own_ref, first_ref, second_ref, emit)
    send_planes(out_ref, to_first_ref, to_second_ref)


def last_update_kernel(
    table_ref, own_ref, first_ref, second_ref, before_ref, inverse_ref, out_ref, moments_ref
):
    def emit(z, rows, lanes, value):
        out_ref[z, rows, lanes] = (
            before_ref[z, rows, lanes] * value * inverse_ref[z, rows, lanes]
        )

    plane_pass(adjoint_coefficient(table_ref), own_ref, first_ref, second_ref, emit)
    total = jnp.zeros((SY, NX), F32)
    for z in range(SZ):
        total += out_ref[z]
    mean = jnp.sum(total, keepdims=True) / LOCAL
    squares = jnp.zeros((SY, NX), F32)
    for z in range(SZ):
        squares += (out_ref[z] - mean) ** 2
    deviation = jnp.sum(squares, keepdims=True)
    moments_ref[...] = jnp.where(iota((DEVICES, 128), 1) == 0, mean, deviation)


def column_pass(value, matrix):
    left = iota((EXT, 128), 1) < 64
    turned = pltpu.roll(value, 64, axis=1)
    edge = turned[:, :128]
    blocks = [jnp.where(left, 0.0, edge)]
    blocks += [turned[:, 128 * j : 128 * (j + 1)] for j in range(1, NX // 128)]
    blocks += [jnp.where(left, edge, 0.0)]
    blocks = [b.astype(BF16) for b in blocks]
    windows = [jnp.concatenate(blocks[j : j + 2], axis=1) for j in range(NX // 128)]
    product = jnp.dot(jnp.concatenate(windows, axis=0), matrix, preferred_element_type=F32)
    product = product[:, :128] + product[:, 128:]
    return jnp.concatenate(
        [product[EXT * j : EXT * (j + 1)] for j in range(NX // 128)], axis=1
    )


def row_pass(matrix, value):
    high, rest = split(value)
    stacked = jnp.concatenate([high, high, rest, jnp.zeros((16, NX), BF16)], axis=0)
    return jnp.dot(matrix, stacked, preferred_element_type=F32)


def ratio_kernel(
    u_ref, u_edge_ref, observed_ref, observed_edge_ref,
    rows_f_ref, rows_a_ref, cols_f_ref, cols_a_ref,
    out_ref, to_first_ref, to_second_ref,
):
    for z in range(SZ):
        extended = jnp.concatenate([u_ref[z], u_edge_ref[z].astype(F32)], axis=0)
        blurred = column_pass(row_pass(rows_f_ref[z], extended), cols_f_ref[z])
        seen = jnp.concatenate([observed_ref[z], observed_edge_ref[z]], axis=0)
        back = column_pass(seen / blurred, cols_a_ref[z])
        out_ref[z] = row_pass(rows_a_ref[z], back)
    send_planes(out_ref, to_first_ref, to_second_ref)


def bricks_kernel(
    tissue_ref, estimate_ref, moments_ref, w1_ref, b1_ref, w2_ref, b2_ref, w3_ref, b3_ref,
    out_ref, listing, stack, hidden, partial, result,
):
    means = moments_ref[:, 0:1]
    centre = jnp.sum(means, axis=0, keepdims=True) / DEVICES
    deviation = jnp.sum(moments_ref[:, 1:2] + LOCAL * (means - centre) ** 2, axis=0, keepdims=True)
    spread = jnp.sqrt(deviation / COUNT + 1e-06)
    out_ref[...] = estimate_ref[...]
    stack[...] = jnp.zeros(stack.shape, F32)

    def note(b, count):
        listing[count] = b
        return count + jnp.where(tissue_ref[b] > 0, 1, 0)

    bricks_across = NX // BX
    many = lax.fori_loop(0, (SY // BY) * bricks_across, note, 0)

    lane = iota((8, 128), 1)
    row = iota((8, 128), 0)
    group = lane // BX
    column = lane % BX
    tall_column = iota((CH, 128), 1) % BX
    tall_group = iota((CH, 128), 1) // BX

    def beside(value, at):
        return (
            jnp.where(at == 0, 0.0, pltpu.roll(value, 1, axis=1)),
            value,
            jnp.where(at == BX - 1, 0.0, pltpu.roll(value, 127, axis=1)),
        )

    @pl.loop(0, many)
    def _(n):
        brick = listing[n]
        down = brick // bricks_across
        over = brick % bricks_across
        lanes = pl.ds(pl.multiple_of(over // 4 * 128, 128), 128)
        quarter = over % 4

        def rows_of(g):
            return pl.ds(pl.multiple_of(down * BY + 8 * g, 8), 8)

        for z in range(SZ):
            brick_plane = jnp.zeros((8, 128), F32)
            for g in range(4):
                block = estimate_ref[z, rows_of(g), lanes]
                turned = pltpu.roll(block, (BX * (g - quarter)) % 128, axis=1)
                brick_plane = jnp.where(group == g, turned, brick_plane)
            normed = ((brick_plane - centre) / spread).astype(BF16).astype(F32)
            before = pltpu.roll(normed, 1, axis=0)
            after = pltpu.roll(normed, 7, axis=0)
            wrapped_before = jnp.where(group == 0, 0.0, pltpu.roll(before, BX, axis=1))
            wrapped_after = jnp.where(group == 3, 0.0, pltpu.roll(after, 128 - BX, axis=1))
            versions = (
                jnp.where(row == 0, wrapped_before, before),
                normed,
                jnp.where(row == 7, wrapped_after, after),
            )
            for b, version in enumerate(versions):
                for c, moved in enumerate(beside(version, column)):
                    for a in range(3):
                        to = z - (a - 1)
                        if 0 <= to < SZ:
                            tap = 9 * a + 3 * b + c
                            stack[pl.ds(to * 256 + tap, 8, stride=32), :] = moved

        @pl.loop(0, SZ)
        def _(z):
            for pair in range(4):
                taps = [
                    stack[pl.ds(pl.multiple_of(z * 256 + (2 * pair + e) * 32, 32), 32), :].astype(BF16)
                    for e in range(2)
                ]
                first = jnp.dot(
                    w1_ref[...], jnp.concatenate(taps, axis=1), preferred_element_type=F32
                )
                first = jnp.maximum(first + b1_ref[...], 0.0)
                for e in range(2):
                    r = 2 * pair + e
                    value = first[:, 128 * e : 128 * (e + 1)]
                    places = [(r + 1, value)]
                    if r == 7:
                        places.append(
                            (0, jnp.where(tall_group == 0, 0.0, pltpu.roll(value, BX, axis=1)))
                        )
                    if r == 0:
                        places.append(
                            (9, jnp.where(tall_group == 3, 0.0, pltpu.roll(value, 128 - BX, axis=1)))
                        )
                    for at, placed in places:
                        moved = jnp.concatenate(beside(placed, tall_column), axis=0)
                        hidden[z, at] = moved.astype(BF16)

        for pair in range(4):
            @pl.loop(0, SZ)
            def _(z):
                taps = [
                    hidden[z, 2 * pair + e : 2 * pair + e + 3].reshape(9 * CH, 128) for e in range(2)
                ]
                partial[z] = jnp.dot(
                    w2_ref[...], jnp.concatenate(taps, axis=1), preferred_element_type=F32
                )

            for z in range(SZ):
                total = partial[z, CH : 2 * CH] + b2_ref[...]
                if z > 0:
                    total += partial[z - 1, :CH]
                if z < SZ - 1:
                    total += partial[z + 1, 2 * CH :]
                second = jnp.maximum(total, 0.0).astype(BF16).astype(F32)
                last = jnp.sum(w3_ref[...] * second, axis=0, keepdims=True) + b3_ref[...]
                result[z, 2 * pair : 2 * pair + 1, :] = last[:, :128]
                result[z, 2 * pair + 1 : 2 * pair + 2, :] = last[:, 128:]

        for z in range(SZ):
            change = result[z] * spread
            for g in range(4):
                turned = pltpu.roll(change, (BX * (quarter - g)) % 128, axis=1)
                out_ref[z, rows_of(g), lanes] += jnp.where(group == quarter, turned, 0.0)


def kernel_tables(psf_taps, psf_index, slab):
    normed = psf_taps / jnp.sum(psf_taps, axis=2, keepdims=True)
    index = lax.dynamic_slice_in_dim(jnp.pad(psf_index, (R, R)), slab * SZ, SPAN, 0)
    plane = slab * SZ - R + jnp.arange(SPAN, dtype=jnp.int32)
    valid = (plane >= 0) & (plane < NZ)
    picked = (index[:, None] == jnp.arange(MODELS, dtype=jnp.int32)[None, :]) & valid[:, None]
    kernels = jnp.sum(jnp.where(picked[:, :, None, None], normed[None], 0.0), axis=1)
    own = kernels[R : R + SZ]
    forward = jnp.pad(own[:, 0], ((0, 0), (0, SZ))).reshape(-1)[: SZ * SPAN].reshape(SZ, SPAN)
    forward = jnp.where(valid[None, :], forward, 0.0)
    wide = SPAN + TAPS - 1
    skewed = jnp.pad(kernels[:, 0], ((0, 0), (0, SPAN))).reshape(-1)[: SPAN * wide]
    adjoint = skewed.reshape(SPAN, wide)[:, TAPS - 1 : TAPS - 1 + SZ]
    table = jnp.concatenate(
        [forward.reshape(-1), adjoint.reshape(-1), own[:, 1].reshape(-1), own[:, 2].reshape(-1)]
    )
    across = jnp.pad(kernels[:, 2], ((0, 2), (0, 1)))
    along = jnp.pad(kernels[:, 1].T, ((0, 1), (0, 128 - SPAN)))
    weight = jnp.pad(adjoint.T, ((0, 0), (0, 128 - SPAN)))
    return table, across, along, weight


def body(observed, psf_taps, psf_index, tissue, w_first, b_first, w_mid, b_mid, w_last, b_last):
    slabs = NZ // SZ
    first_pairs = [(i, i ^ 1) for i in range(slabs)]
    second_pairs = [(i, ((((i + 1) % slabs) ^ 1) - 1) % slabs) for i in range(slabs)]
    swap = [(0, 1), (1, 0)]
    volume = shape((SZ, SY, NX), F32)
    planes = shape((R, SY, NX), BF16)

    def beside(first, second):
        return lax.ppermute(first, "gz", first_pairs), lax.ppermute(second, "gz", second_pairs)

    first, second, edge = call(
        prepare_kernel, [planes, planes, shape((SZ, HALO, NX), F32)], [observed], [VMEM]
    )
    first, second = beside(first, second)
    observed_edge = lax.ppermute(edge, "gy", swap)

    table, across, along, weight = kernel_tables(psf_taps, psf_index, lax.axis_index("gz"))
    rows_f, rows_a, cols_f, cols_a, inverse = call(
        setup_kernel,
        [
            shape((SZ, EXT, 256), BF16),
            shape((SZ, SY, 256), BF16),
            shape((SZ, 256, 256), BF16),
            shape((SZ, 256, 256), BF16),
            volume,
        ],
        [table, across, along, weight],
        [SMEM, VMEM, VMEM, VMEM],
        flops=100_000_000,
    )

    estimate = observed
    for turn in range(2):
        u, u_edge = call(
            forward_planes_kernel,
            [volume, shape((SZ, HALO, NX), BF16)],
            [table, estimate, first, second],
            [SMEM, VMEM, VMEM, VMEM],
            flops=30 * SZ * SY * NX,
        )
        u_edge = lax.ppermute(u_edge, "gy", swap)
        q, first, second = call(
            ratio_kernel,
            [volume, planes, planes],
            [u, u_edge, observed, observed_edge, rows_f, rows_a, cols_f, cols_a],
            [VMEM] * 8,
            flops=1_000_000_000,
        )
        first, second = beside(first, second)
        ins = [table, q, first, second, estimate, inverse]
        specs = [SMEM] + [VMEM] * 5
        if turn == 0:
            estimate, first, second = call(
                update_kernel, [volume, planes, planes], ins, specs, flops=30 * SZ * SY * NX
            )
            first, second = beside(first, second)
        else:
            estimate, moments = call(
                last_update_kernel,
                [volume, shape((DEVICES, 128), F32)],
                ins,
                specs,
                flops=30 * SZ * SY * NX,
            )
    moments = lax.all_to_all(moments, ("gz", "gy"), 0, 0, tiled=True)

    w1 = jnp.pad(w_first, ((0, 0), (0, CH - 27)))
    w2 = w_mid.reshape(3, 9, CH, CH).transpose(0, 2, 1, 3).reshape(3 * CH, 9 * CH)
    (restored,) = call(
        bricks_kernel,
        [volume],
        [
            tissue.reshape(-1), estimate, moments, w1, b_first[:, None], w2, b_mid[:, None],
            w_last.astype(F32)[:, None], b_last[:, None],
        ],
        [SMEM] + [VMEM] * 8,
        scratch=[
            pltpu.SMEM((64,), jnp.int32),
            pltpu.VMEM((SZ * 256, 128), F32),
            pltpu.VMEM((SZ, 10, 3 * CH, 128), BF16),
            pltpu.VMEM((SZ, 3 * CH, 256), F32),
            pltpu.VMEM((SZ, 8, 128), F32),
        ],
        flops=1_000_000_000,
    )
    return restored


def solution(mesh):
    return jax.shard_map(
        body,
        mesh=mesh,
        in_specs=(P("gz", "gy", None), P(), P(), P("gz", "gy", None), P(), P(), P(), P(), P(), P()),
        out_specs=P("gz", "gy", None),
        check_vma=False,
    )
```

```python
import jax
import jax.numpy as jnp
from jax import lax
from jax.experimental import pallas as pl
from jax.experimental.pallas import tpu as pltpu
from jax.sharding import PartitionSpec as P

F32 = jnp.float32
BF16 = jnp.bfloat16
SZ, SY, NX = 8, 64, 512
NZ, NY = 512, 128
TAPS, R = 15, 7
HALO = 16
EXT = SY + HALO
MODELS = 8
BY, BX = 32, 32
CH = 32
ACROSS = NX // BX
BRICKS = (SY // BY) * ACROSS
MOST = 3
SPAN = SZ + 2 * R
COUNT = float(NZ * NY * NX)
LOCAL = float(SZ * SY * NX)
DEVICES = 128
AT_FORWARD = 0
AT_ADJOINT = SZ * SPAN
AT_ROWS = 2 * SZ * SPAN
AT_COLUMNS = AT_ROWS + SZ * TAPS
MIB = 1024 * 1024

VMEM = pl.BlockSpec(memory_space=pltpu.VMEM)
SMEM = pl.BlockSpec(memory_space=pltpu.SMEM)


def iota(shape, axis):
    return lax.broadcasted_iota(jnp.int32, shape, axis)


def call(kernel, outs, ins, specs, scratch=(), flops=0, limit=24):
    moved = sum(x.size * x.dtype.itemsize for x in list(ins) + list(outs))
    return pl.pallas_call(
        kernel,
        out_shape=outs,
        in_specs=specs,
        out_specs=[VMEM] * len(outs),
        scratch_shapes=scratch,
        compiler_params=pltpu.CompilerParams(vmem_limit_bytes=limit * MIB),
        cost_estimate=pl.CostEstimate(flops=flops, bytes_accessed=moved, transcendentals=0),
    )(*ins)


def shape(dims, dtype):
    return jax.ShapeDtypeStruct(dims, dtype)


def send_planes(volume_ref, first_ref, second_ref):
    even = 1 - lax.axis_index("gz") % 2

    @pl.loop(0, R)
    def _(k):
        first_ref[k] = volume_ref[k + even].astype(BF16)
        second_ref[k] = volume_ref[k + 1 - even].astype(BF16)


def edge_rows(volume, rows, gy):
    start = pl.multiple_of((1 - gy) * (SY - rows), rows)
    return volume[:, pl.ds(start, rows), :]


def prepare_kernel(observed_ref, first_ref, second_ref, edge_ref):
    gy = lax.axis_index("gy")
    send_planes(observed_ref, first_ref, second_ref)
    edge_ref[...] = edge_rows(observed_ref, HALO, gy)


def split(value):
    high = value.astype(BF16)
    return high, (value - high.astype(F32)).astype(BF16)


def setup_kernel(
    table_ref, kx_ref, kyt_ref, weight_ref, rows_f_ref, rows_a_ref, cols_f_ref, cols_a_ref, inverse_ref
):
    gy = lax.axis_index("gy")

    def place(index):
        return jnp.where(index < SY, index, jnp.where(gy == 0, index, index - EXT))

    lane = iota((EXT, 256), 1)
    piece = lane // EXT
    inside = place(lane - piece * EXT)
    outside = place(iota((EXT, 256), 0))
    used = piece < 3
    tap_f = jnp.where(used, inside - outside + R, -1)
    tap_a = jnp.where(used, outside - inside + R, -1)[:SY]
    low = piece == 1
    source = iota((256, 128), 0)
    target = iota((256, 128), 1)
    tap_cf = source - target - (64 - R)
    tap_ca = target - source + (64 + R)

    @pl.loop(0, SZ)
    def _(z):
        def table(taps, at):
            total = jnp.zeros(taps.shape, F32)
            for t in range(TAPS):
                total = jnp.where(taps == t, table_ref[at + z * TAPS + t], total)
            return total

        def halves(value, is_low):
            high = value.astype(BF16).astype(F32)
            return jnp.where(is_low, value - high, high).astype(BF16)

        rows_f_ref[z] = halves(table(tap_f, AT_ROWS), low)
        rows_a_ref[z] = halves(table(tap_a, AT_ROWS), low[:SY])
        for taps, out in ((tap_cf, cols_f_ref), (tap_ca, cols_a_ref)):
            high, rest = split(table(taps, AT_COLUMNS))
            out[z, :, :128] = high
            out[z, :, 128:] = rest

    column = iota((1, NX), 1)
    row = iota((SY, 1), 0) + gy * SY
    across = jnp.zeros((24, NX), F32)
    along = jnp.zeros((SY, 128), F32)
    for t in range(TAPS):
        at_x = column + R - t
        at_y = row + R - t
        across += jnp.where((at_x >= 0) & (at_x < NX), kx_ref[:, t : t + 1], 0.0)
        along += jnp.where((at_y >= 0) & (at_y < NY), kyt_ref[t : t + 1, :], 0.0)
    across = jnp.concatenate([across, jnp.zeros((104, NX), F32)], axis=0)
    for z in range(SZ):
        norm = jnp.dot(
            along * weight_ref[z : z + 1, :],
            across,
            precision=lax.Precision.HIGHEST,
            preferred_element_type=F32,
        )
        inverse_ref[z] = 1.0 / norm


def plane_pass(coefficient, own_ref, first_ref, second_ref, emit):
    even = lax.axis_index("gz") % 2 == 0
    high, wide = 16, 256

    def run(low_ref, high_ref):
        @pl.loop(0, SY // high)
        def _(block):
            rows = pl.ds(pl.multiple_of(block * high, high), high)
            for part in range(NX // wide):
                lanes = pl.ds(part * wide, wide)
                planes = [low_ref[k, rows, lanes].astype(F32) for k in range(R)]
                planes += [own_ref[k, rows, lanes] for k in range(SZ)]
                planes += [high_ref[k, rows, lanes].astype(F32) for k in range(R)]
                for z in range(SZ):
                    terms = [coefficient(z, j) * planes[j] for j in range(z, z + TAPS)]
                    while len(terms) > 1:
                        terms = [sum(terms[i : i + 2]) for i in range(0, len(terms), 2)]
                    emit(z, rows, lanes, terms[0])

    @pl.when(even)
    def _():
        run(second_ref, first_ref)

    @pl.when(jnp.logical_not(even))
    def _():
        run(first_ref, second_ref)


def forward_planes_kernel(
    table_ref, own_ref, first_ref, second_ref, inverse_ref, out_ref, edge_ref
):
    del inverse_ref
    def emit(z, rows, lanes, value):
        out_ref[z, rows, lanes] = value

    plane_pass(
        lambda z, j: table_ref[AT_FORWARD + z * SPAN + j], own_ref, first_ref, second_ref, emit
    )
    edge_ref[...] = edge_rows(out_ref, HALO, lax.axis_index("gy")).astype(BF16)


def adjoint_coefficient(table_ref):
    return lambda z, j: table_ref[AT_ADJOINT + j * SZ + z]


def update_kernel(
    table_ref, own_ref, first_ref, second_ref, before_ref, inverse_ref, out_ref, to_first_ref, to_second_ref
):
    def emit(z, rows, lanes, value):
        out_ref[z, rows, lanes] = (
            before_ref[z, rows, lanes] * value * inverse_ref[z, rows, lanes]
        )

    plane_pass(adjoint_coefficient(table_ref), own_ref, first_ref, second_ref, emit)
    send_planes(out_ref, to_first_ref, to_second_ref)


def last_update_kernel(
    table_ref, own_ref, first_ref, second_ref, before_ref, inverse_ref, out_ref, moments_ref
):
    def emit(z, rows, lanes, value):
        out_ref[z, rows, lanes] = (
            before_ref[z, rows, lanes] * value * inverse_ref[z, rows, lanes]
        )

    plane_pass(adjoint_coefficient(table_ref), own_ref, first_ref, second_ref, emit)
    total = jnp.zeros((SY, NX), F32)
    for z in range(SZ):
        total += out_ref[z]
    mean = jnp.sum(total, keepdims=True) / LOCAL
    squares = jnp.zeros((SY, NX), F32)
    for z in range(SZ):
        squares += (out_ref[z] - mean) ** 2
    deviation = jnp.sum(squares, keepdims=True)
    moments_ref[...] = jnp.where(iota((DEVICES, 128), 1) == 0, mean, deviation)


def column_pass(value, matrix):
    left = iota((EXT, 128), 1) < 64
    turned = pltpu.roll(value, 64, axis=1)
    edge = turned[:, :128]
    blocks = [jnp.where(left, 0.0, edge)]
    blocks += [turned[:, 128 * j : 128 * (j + 1)] for j in range(1, NX // 128)]
    blocks += [jnp.where(left, edge, 0.0)]
    blocks = [b.astype(BF16) for b in blocks]
    windows = [jnp.concatenate(blocks[j : j + 2], axis=1) for j in range(NX // 128)]
    product = jnp.dot(jnp.concatenate(windows, axis=0), matrix, preferred_element_type=F32)
    product = product[:, :128] + product[:, 128:]
    return jnp.concatenate(
        [product[EXT * j : EXT * (j + 1)] for j in range(NX // 128)], axis=1
    )


def row_pass(matrix, value):
    high, rest = split(value)
    stacked = jnp.concatenate([high, high, rest, jnp.zeros((16, NX), BF16)], axis=0)
    return jnp.dot(matrix, stacked, preferred_element_type=F32)


def ratio_kernel(
    u_ref, u_edge_ref, observed_ref, observed_edge_ref,
    rows_f_ref, rows_a_ref, cols_f_ref, cols_a_ref,
    out_ref, to_first_ref, to_second_ref,
):
    for z in range(SZ):
        extended = jnp.concatenate([u_ref[z], u_edge_ref[z].astype(F32)], axis=0)
        blurred = column_pass(row_pass(rows_f_ref[z], extended), cols_f_ref[z])
        seen = jnp.concatenate([observed_ref[z], observed_edge_ref[z]], axis=0)
        back = column_pass(seen / blurred, cols_a_ref[z])
        out_ref[z] = row_pass(rows_a_ref[z], back)
    send_planes(out_ref, to_first_ref, to_second_ref)


def beside(value, at):
    return (
        jnp.where(at == 0, 0.0, pltpu.roll(value, 1, axis=1)),
        value,
        jnp.where(at == BX - 1, 0.0, pltpu.roll(value, 127, axis=1)),
    )


def note_bricks(tissue_ref, listing):
    def note(b, count):
        listing[count] = b
        return count + jnp.where(tissue_ref[b] > 0, 1, 0)

    return lax.fori_loop(0, BRICKS, note, 0)


def place_of(brick):
    down = brick // ACROSS
    over = brick % ACROSS

    def rows_of(g):
        return pl.ds(pl.multiple_of(down * BY + 8 * g, 8), 8)

    return rows_of, pl.ds(pl.multiple_of(over // 4 * 128, 128), 128), over % 4


def first_kernel(tissue_ref, estimate_ref, mean_ref, w1_ref, raw_ref, ones_ref, listing, stack):
    many = note_bricks(tissue_ref, listing)
    mean = mean_ref[0:1, 0:1]
    stack[...] = jnp.zeros(stack.shape, F32)
    lane = iota((8, 128), 1)
    row = iota((8, 128), 0)
    group = lane // BX
    column = lane % BX

    def fill(z, plane):
        before = pltpu.roll(plane, 1, axis=0)
        after = pltpu.roll(plane, 7, axis=0)
        wrapped_before = jnp.where(group == 0, 0.0, pltpu.roll(before, BX, axis=1))
        wrapped_after = jnp.where(group == 3, 0.0, pltpu.roll(after, 128 - BX, axis=1))
        versions = (
            jnp.where(row == 0, wrapped_before, before),
            plane,
            jnp.where(row == 7, wrapped_after, after),
        )
        for b, version in enumerate(versions):
            for c, moved in enumerate(beside(version, column)):
                for a in range(3):
                    to = z - (a - 1)
                    if 0 <= to < SZ:
                        tap = 9 * a + 3 * b + c
                        stack[pl.ds(to * 256 + tap, 8, stride=32), :] = moved

    def convolve(store):
        for z in range(SZ):
            for pair in range(4):
                at = z * 256 + 2 * pair * 32
                taps = [stack[at + 32 * e : at + 32 * (e + 1), :].astype(BF16) for e in range(2)]
                store(
                    z,
                    pair,
                    jnp.dot(
                        w1_ref[...], jnp.concatenate(taps, axis=1), preferred_element_type=F32
                    ),
                )

    for z in range(SZ):
        fill(z, jnp.ones((8, 128), F32))

    def keep_ones(z, pair, value):
        ones_ref[z, pair] = value

    convolve(keep_ones)

    @pl.loop(0, many)
    def _(n):
        rows_of, lanes, quarter = place_of(listing[n])
        for z in range(SZ):
            plane = jnp.zeros((8, 128), F32)
            for g in range(4):
                block = estimate_ref[z, rows_of(g), lanes]
                turned = pltpu.roll(block, (BX * (g - quarter)) % 128, axis=1)
                plane = jnp.where(group == g, turned, plane)
            fill(z, plane - mean)

        def keep(z, pair, value):
            raw_ref[n, z, pair] = value

        convolve(keep)


def bricks_kernel(
    tissue_ref, estimate_ref, mean_ref, moments_ref, raw_ref, ones_ref,
    b1_ref, w2_ref, b2_ref, w3_ref, b3_ref,
    out_ref, listing, hidden, partial, result,
):
    means = moments_ref[:, 0:1]
    centre = jnp.sum(means, axis=0, keepdims=True) / DEVICES
    deviation = jnp.sum(moments_ref[:, 1:2] + LOCAL * (means - centre) ** 2, axis=0, keepdims=True)
    spread = jnp.sqrt(deviation / COUNT + 1e-06)
    scale = 1.0 / spread
    offset = mean_ref[0:1, 0:1] - centre
    out_ref[...] = estimate_ref[...]
    many = note_bricks(tissue_ref, listing)
    group = iota((8, 128), 1) // BX
    tall_column = iota((CH, 128), 1) % BX
    tall_group = iota((CH, 128), 1) // BX

    @pl.loop(0, many)
    def _(n):
        rows_of, lanes, quarter = place_of(listing[n])

        for z in range(SZ):
            for pair in range(4):
                first = (raw_ref[n, z, pair] + offset * ones_ref[z, pair]) * scale + b1_ref[...]
                first = jnp.maximum(first, 0.0)
                for e in range(2):
                    r = 2 * pair + e
                    value = first[:, 128 * e : 128 * (e + 1)]
                    places = [(r + 1, value)]
                    if r == 7:
                        places.append(
                            (0, jnp.where(tall_group == 0, 0.0, pltpu.roll(value, BX, axis=1)))
                        )
                    if r == 0:
                        places.append(
                            (9, jnp.where(tall_group == 3, 0.0, pltpu.roll(value, 128 - BX, axis=1)))
                        )
                    for at, placed in places:
                        moved = jnp.concatenate(beside(placed, tall_column), axis=0)
                        hidden[z, at] = moved.astype(BF16)

        for z in range(SZ):
            for pair in range(4):
                taps = [
                    hidden[z, 2 * pair + e : 2 * pair + e + 3].reshape(9 * CH, 128) for e in range(2)
                ]
                partial[z, pair] = jnp.dot(
                    w2_ref[...], jnp.concatenate(taps, axis=1), preferred_element_type=F32
                )

        for z in range(SZ):
            for pair in range(4):
                total = partial[z, pair, CH : 2 * CH] + b2_ref[...]
                if z > 0:
                    total += partial[z - 1, pair, :CH]
                if z < SZ - 1:
                    total += partial[z + 1, pair, 2 * CH :]
                second = jnp.maximum(total, 0.0).astype(BF16).astype(F32)
                last = jnp.sum(w3_ref[...] * second, axis=0, keepdims=True) + b3_ref[...]
                result[z, 2 * pair : 2 * pair + 1, :] = last[:, :128]
                result[z, 2 * pair + 1 : 2 * pair + 2, :] = last[:, 128:]

        for z in range(SZ):
            change = result[z] * spread
            for g in range(4):
                turned = pltpu.roll(change, (BX * (quarter - g)) % 128, axis=1)
                out_ref[z, rows_of(g), lanes] += jnp.where(group == quarter, turned, 0.0)


def kernel_tables(psf_taps, psf_index, slab):
    normed = psf_taps / jnp.sum(psf_taps, axis=2, keepdims=True)
    index = lax.dynamic_slice_in_dim(jnp.pad(psf_index, (R, R)), slab * SZ, SPAN, 0)
    plane = slab * SZ - R + jnp.arange(SPAN, dtype=jnp.int32)
    valid = (plane >= 0) & (plane < NZ)
    picked = (index[:, None] == jnp.arange(MODELS, dtype=jnp.int32)[None, :]) & valid[:, None]
    kernels = jnp.sum(jnp.where(picked[:, :, None, None], normed[None], 0.0), axis=1)
    own = kernels[R : R + SZ]
    forward = jnp.pad(own[:, 0], ((0, 0), (0, SZ))).reshape(-1)[: SZ * SPAN].reshape(SZ, SPAN)
    forward = jnp.where(valid[None, :], forward, 0.0)
    wide = SPAN + TAPS - 1
    skewed = jnp.pad(kernels[:, 0], ((0, 0), (0, SPAN))).reshape(-1)[: SPAN * wide]
    adjoint = skewed.reshape(SPAN, wide)[:, TAPS - 1 : TAPS - 1 + SZ]
    table = jnp.concatenate(
        [forward.reshape(-1), adjoint.reshape(-1), own[:, 1].reshape(-1), own[:, 2].reshape(-1)]
    )
    across = jnp.pad(kernels[:, 2], ((0, 2), (0, 1)))
    along = jnp.pad(kernels[:, 1].T, ((0, 1), (0, 128 - SPAN)))
    weight = jnp.pad(adjoint.T, ((0, 0), (0, 128 - SPAN)))
    return table, across, along, weight


def body(observed, psf_taps, psf_index, tissue, w_first, b_first, w_mid, b_mid, w_last, b_last):
    slabs = NZ // SZ
    first_pairs = [(i, i ^ 1) for i in range(slabs)]
    second_pairs = [(i, ((i + 1) ^ 1) - 1) for i in range(1, slabs - 1)]
    swap = [(0, 1), (1, 0)]
    volume = shape((SZ, SY, NX), F32)
    planes = shape((R, SY, NX), BF16)

    def beside(first, second):
        return lax.ppermute(first, "gz", first_pairs), lax.ppermute(second, "gz", second_pairs)

    first, second, edge = call(
        prepare_kernel, [planes, planes, shape((SZ, HALO, NX), F32)], [observed], [VMEM]
    )
    first, second = beside(first, second)
    observed_edge = lax.ppermute(edge, "gy", swap)

    table, across, along, weight = kernel_tables(psf_taps, psf_index, lax.axis_index("gz"))
    rows_f, rows_a, cols_f, cols_a, inverse = call(
        setup_kernel,
        [
            shape((SZ, EXT, 256), BF16),
            shape((SZ, SY, 256), BF16),
            shape((SZ, 256, 256), BF16),
            shape((SZ, 256, 256), BF16),
            volume,
        ],
        [table, across, along, weight],
        [SMEM, VMEM, VMEM, VMEM],
        flops=100_000_000,
    )

    estimate = observed
    for turn in range(2):
        u, u_edge = call(
            forward_planes_kernel,
            [volume, shape((SZ, HALO, NX), BF16)],
            [table, estimate, first, second, inverse],
            [SMEM] + [VMEM] * 4,
            flops=30 * SZ * SY * NX,
        )
        u_edge = lax.ppermute(u_edge, "gy", swap)
        q, first, second = call(
            ratio_kernel,
            [volume, planes, planes],
            [u, u_edge, observed, observed_edge, rows_f, rows_a, cols_f, cols_a],
            [VMEM] * 8,
            flops=1_000_000_000,
        )
        first, second = beside(first, second)
        ins = [table, q, first, second, estimate, inverse]
        specs = [SMEM] + [VMEM] * 5
        if turn == 0:
            estimate, first, second = call(
                update_kernel, [volume, planes, planes], ins, specs, flops=30 * SZ * SY * NX
            )
            first, second = beside(first, second)
        else:
            estimate, own_moments = call(
                last_update_kernel,
                [volume, shape((DEVICES, 128), F32)],
                ins,
                specs,
                flops=30 * SZ * SY * NX,
            )
    moments = lax.all_to_all(own_moments, ("gz", "gy"), 0, 0, tiled=True)

    w1 = jnp.pad(w_first, ((0, 0), (0, CH - 27)))
    w2 = w_mid.reshape(3, 9, CH, CH).transpose(0, 2, 1, 3).reshape(3 * CH, 9 * CH)
    flags = tissue.reshape(-1)
    raw, ones = call(
        first_kernel,
        [shape((MOST, SZ, 4, CH, 256), F32), shape((SZ, 4, CH, 256), F32)],
        [flags, estimate, own_moments, w1],
        [SMEM] + [VMEM] * 3,
        scratch=[pltpu.SMEM((64,), jnp.int32), pltpu.VMEM((SZ * 256, 128), F32)],
        flops=100_000_000,
    )
    (restored,) = call(
        bricks_kernel,
        [volume],
        [
            flags, estimate, own_moments, moments, raw, ones, b_first[:, None], w2, b_mid[:, None],
            w_last.astype(F32)[:, None], b_last[:, None],
        ],
        [SMEM] + [VMEM] * 10,
        scratch=[
            pltpu.SMEM((64,), jnp.int32),
            pltpu.VMEM((SZ, 10, 3 * CH, 128), BF16),
            pltpu.VMEM((SZ, 4, 3 * CH, 256), F32),
            pltpu.VMEM((SZ, 8, 128), F32),
        ],
        flops=1_000_000_000,
    )
    return restored


def solution(mesh):
    return jax.shard_map(
        body,
        mesh=mesh,
        in_specs=(P("gz", "gy", None), P(), P(), P("gz", "gy", None), P(), P(), P(), P(), P(), P()),
        out_specs=P("gz", "gy", None),
        check_vma=False,
    )
```

```python
import jax
import jax.numpy as jnp
from jax import lax
from jax.experimental import pallas as pl
from jax.experimental.pallas import tpu as pltpu
from jax.sharding import PartitionSpec as P

F32 = jnp.float32
BF16 = jnp.bfloat16
SZ, SY, NX = 8, 64, 512
NZ, NY = 512, 128
TAPS, R = 15, 7
HALO = 16
EXT = SY + HALO
MODELS = 8
BY, BX = 32, 32
CH = 32
ACROSS = NX // BX
BRICKS = (SY // BY) * ACROSS
TALL = 64
WIDE = NX + 128
SPAN = SZ + 2 * R
COUNT = float(NZ * NY * NX)
LOCAL = float(SZ * SY * NX)
DEVICES = 128
AT_FORWARD = 0
AT_ADJOINT = SZ * SPAN
MIB = 1024 * 1024

VMEM = pl.BlockSpec(memory_space=pltpu.VMEM)
SMEM = pl.BlockSpec(memory_space=pltpu.SMEM)


def iota(shape, axis):
    return lax.broadcasted_iota(jnp.int32, shape, axis)


def call(kernel, outs, ins, specs, out_specs=None, scratch=(), flops=0, limit=24):
    moved = sum(x.size * x.dtype.itemsize for x in list(ins) + list(outs))
    return pl.pallas_call(
        kernel,
        out_shape=outs,
        in_specs=specs,
        out_specs=out_specs or [VMEM] * len(outs),
        scratch_shapes=scratch,
        compiler_params=pltpu.CompilerParams(vmem_limit_bytes=limit * MIB),
        cost_estimate=pl.CostEstimate(flops=flops, bytes_accessed=moved, transcendentals=0),
    )(*ins)


def shape(dims, dtype):
    return jax.ShapeDtypeStruct(dims, dtype)


def send_planes(volume_ref, first_ref, second_ref):
    even = 1 - lax.axis_index("gz") % 2

    @pl.loop(0, R)
    def _(k):
        first_ref[k] = volume_ref[k + even].astype(BF16)
        second_ref[k] = volume_ref[k + 1 - even].astype(BF16)


def edge_rows(volume, rows, gy):
    start = pl.multiple_of((1 - gy) * (SY - rows), rows)
    return volume[:, pl.ds(start, rows), :]


def shift_columns(plane):
    left = iota((plane.shape[0], 128), 1) < 64
    turned = pltpu.roll(plane, 64, axis=1)
    edge = turned[:, :128]
    return jnp.concatenate(
        [jnp.where(left, 0.0, edge), turned[:, 128:], jnp.where(left, edge, 0.0)], axis=1
    )


def prepare_kernel(observed_ref, first_ref, second_ref, edge_ref):
    gy = lax.axis_index("gy")
    send_planes(observed_ref, first_ref, second_ref)
    edge = edge_rows(observed_ref, HALO, gy)
    for z in range(SZ):
        edge_ref[z] = shift_columns(edge[z])


def split(value):
    high = value.astype(BF16)
    return high, (value - high.astype(F32)).astype(BF16)


def setup_kernel(
    taps_ref, index_ref, rows_ref, observed_ref,
    table_ref, rows_f_ref, rows_a_ref, cols_f_ref, cols_a_ref, inverse_ref, shifted_ref,
    picked_y, picked_x, scaled,
):
    gy = lax.axis_index("gy")
    base = lax.axis_index("gz") * SZ - R

    def model(j):
        plane = base + j
        valid = (plane >= 0) & (plane < NZ)
        return index_ref[jnp.clip(plane, 0, NZ - 1)], valid

    picked_y[...] = jnp.zeros(picked_y.shape, F32)
    picked_x[...] = jnp.zeros(picked_x.shape, F32)
    for j in range(SPAN):
        which, valid = model(j)
        keep = jnp.where(valid, 1.0, 0.0)
        picked_y[j : j + 1, :] = rows_ref[pl.ds(MODELS + which, 1), :] * keep
        picked_x[j : j + 1, :] = rows_ref[pl.ds(2 * MODELS + which, 1), :] * keep
        for z in range(SZ):
            if 0 <= j - z < TAPS:
                own, _ = model(z + R)
                table_ref[AT_FORWARD + z * SPAN + j] = taps_ref[own * TAPS + j - z] * keep
                table_ref[AT_ADJOINT + j * SZ + z] = (
                    taps_ref[which * TAPS + z + TAPS - 1 - j] * keep
                )

    def place(index):
        return jnp.where(index < SY, index, jnp.where(gy == 0, index, index - EXT))

    lane = iota((EXT, 256), 1)
    piece = lane // EXT
    inside = place(lane - piece * EXT)
    outside = place(iota((EXT, 256), 0))
    used = piece < 3
    tap_f = jnp.where(used, inside - outside + R, -1)
    tap_a = jnp.where(used, outside - inside + R, -1)[:SY]
    low = piece == 1
    source = iota((256, 128), 0)
    target = iota((256, 128), 1)
    tap_cf = source - target - (64 - R)
    tap_ca = target - source + (64 + R)

    @pl.loop(0, SZ)
    def _(z):
        own, _ = model(z + R)

        def table(taps, axis):
            at = (axis * MODELS + own) * TAPS
            total = jnp.zeros(taps.shape, F32)
            for t in range(TAPS):
                total = jnp.where(taps == t, taps_ref[at + t], total)
            return total

        def halves(value, is_low):
            high = value.astype(BF16).astype(F32)
            return jnp.where(is_low, value - high, high).astype(BF16)

        rows_f_ref[z] = halves(table(tap_f, 1), low)
        rows_a_ref[z] = halves(table(tap_a, 1), low[:SY])
        for taps, out in ((tap_cf, cols_f_ref), (tap_ca, cols_a_ref)):
            high, rest = split(table(taps, 2))
            out[z, :, :128] = high
            out[z, :, 128:] = rest
        shifted_ref[z] = shift_columns(observed_ref[z])

    def exact(left, right, contract):
        return lax.dot_general(
            left, right, (contract, ((), ())),
            precision=lax.Precision.HIGHEST, preferred_element_type=F32,
        )

    at_y = iota((SY, 128), 0) + gy * SY + R - iota((SY, 128), 1)
    at_x = iota((128, NX), 1) + R - iota((128, NX), 0)
    along = exact(
        jnp.where((at_y >= 0) & (at_y < NY), 1.0, 0.0), picked_y[...], ((1,), (1,))
    )
    across = exact(picked_x[...], jnp.where((at_x >= 0) & (at_x < NX), 1.0, 0.0), ((1,), (0,)))
    for z in range(SZ):
        scaled[...] = jnp.zeros(scaled.shape, F32)
        for j in range(z, z + TAPS):
            scaled[j : j + 1, :] = across[j : j + 1, :] * table_ref[AT_ADJOINT + j * SZ + z]
        inverse_ref[z] = 1.0 / exact(along, scaled[...], ((1,), (0,)))


def plane_pass(coefficient, own_ref, first_ref, second_ref, emit):
    even = lax.axis_index("gz") % 2 == 0
    high, wide = 16, 256

    def run(low_ref, high_ref):
        @pl.loop(0, SY // high)
        def _(block):
            rows = pl.ds(pl.multiple_of(block * high, high), high)
            for part in range(NX // wide):
                lanes = pl.ds(part * wide, wide)
                planes = [low_ref[k, rows, lanes].astype(F32) for k in range(R)]
                planes += [own_ref[k, rows, lanes] for k in range(SZ)]
                planes += [high_ref[k, rows, lanes].astype(F32) for k in range(R)]
                for z in range(SZ):
                    terms = [coefficient(z, j) * planes[j] for j in range(z, z + TAPS)]
                    while len(terms) > 1:
                        terms = [sum(terms[i : i + 2]) for i in range(0, len(terms), 2)]
                    emit(z, rows, lanes, terms[0])

    @pl.when(even)
    def _():
        run(second_ref, first_ref)

    @pl.when(jnp.logical_not(even))
    def _():
        run(first_ref, second_ref)


def forward_planes_kernel(
    table_ref, own_ref, first_ref, second_ref, inverse_ref, out_ref, edge_ref
):
    del inverse_ref
    def emit(z, rows, lanes, value):
        out_ref[z, rows, lanes] = value

    plane_pass(
        lambda z, j: table_ref[AT_FORWARD + z * SPAN + j], own_ref, first_ref, second_ref, emit
    )
    edge_ref[...] = edge_rows(out_ref, HALO, lax.axis_index("gy")).astype(BF16)


def adjoint_coefficient(table_ref):
    return lambda z, j: table_ref[AT_ADJOINT + j * SZ + z]


def update_kernel(
    table_ref, own_ref, first_ref, second_ref, before_ref, inverse_ref, out_ref, to_first_ref, to_second_ref
):
    def emit(z, rows, lanes, value):
        out_ref[z, rows, lanes] = (
            before_ref[z, rows, lanes] * value * inverse_ref[z, rows, lanes]
        )

    plane_pass(adjoint_coefficient(table_ref), own_ref, first_ref, second_ref, emit)
    send_planes(out_ref, to_first_ref, to_second_ref)


def last_update_kernel(
    table_ref, own_ref, first_ref, second_ref, before_ref, inverse_ref, out_ref, moments_ref
):
    def emit(z, rows, lanes, value):
        out_ref[z, rows, lanes] = (
            before_ref[z, rows, lanes] * value * inverse_ref[z, rows, lanes]
        )

    plane_pass(adjoint_coefficient(table_ref), own_ref, first_ref, second_ref, emit)
    total = jnp.zeros((SY, NX), F32)
    for z in range(SZ):
        total += out_ref[z]
    mean = jnp.sum(total, keepdims=True) / LOCAL
    squares = jnp.zeros((SY, NX), F32)
    for z in range(SZ):
        squares += (out_ref[z] - mean) ** 2
    deviation = jnp.sum(squares, keepdims=True)
    moments_ref[...] = jnp.where(iota((DEVICES, 128), 1) == 0, mean, deviation)


def windows_of(blocks):
    blocks = [b.astype(BF16) for b in blocks]
    pairs = [jnp.concatenate(blocks[j : j + 2], axis=1) for j in range(len(blocks) - 1)]
    return jnp.concatenate(pairs, axis=0)


def column_pass(blocks, matrix):
    product = jnp.dot(windows_of(blocks), matrix, preferred_element_type=F32)
    product = product[:, :128] + product[:, 128:]
    return [product[EXT * j : EXT * (j + 1)] for j in range(len(blocks) - 1)]


def row_pass(matrix, value):
    high, rest = split(value)
    stacked = jnp.concatenate([high, high, rest, jnp.zeros((16, NX), BF16)], axis=0)
    return jnp.dot(matrix, stacked, preferred_element_type=F32)


def ratio_kernel(
    u_ref, u_edge_ref, observed_ref, observed_edge_ref,
    rows_f_ref, rows_a_ref, cols_f_ref, cols_a_ref,
    out_ref, to_first_ref, to_second_ref,
    wide, wider,
):
    columns = NX // 128
    left = iota((EXT, 128), 1) < 64
    none = jnp.zeros((EXT, 128), F32)
    for z in range(SZ):
        extended = jnp.concatenate([u_ref[z], u_edge_ref[z].astype(F32)], axis=0)
        wide[z] = row_pass(rows_f_ref[z], extended)
    for z in range(SZ):
        blocks = [wide[z, :, 128 * j : 128 * (j + 1)] for j in range(columns)]
        blurred = column_pass([none] + blocks + [none], cols_f_ref[z])
        blurred[0] = jnp.where(left, 1.0, blurred[0])
        blurred[-1] = jnp.where(left, blurred[-1], 1.0)
        for j, block in enumerate(blurred):
            lanes = slice(128 * j, 128 * (j + 1))
            wider[z, :SY, lanes] = observed_ref[z, :, lanes] / block[:SY]
            wider[z, SY:, lanes] = observed_edge_ref[z, :, lanes] / block[SY:]
    for z in range(SZ):
        blocks = [wider[z, :, 128 * j : 128 * (j + 1)] for j in range(columns + 1)]
        wide[z] = jnp.concatenate(column_pass(blocks, cols_a_ref[z]), axis=1)
    for z in range(SZ):
        out_ref[z] = row_pass(rows_a_ref[z], wide[z])
    send_planes(out_ref, to_first_ref, to_second_ref)


def note_bricks(tissue_ref, listing):
    def note(b, count):
        listing[count] = b
        return count + jnp.where(tissue_ref[b] > 0, 1, 0)

    return lax.fori_loop(0, BRICKS, note, 0)


def place_of(brick):
    down = brick // ACROSS
    over = brick % ACROSS

    def rows_of(g):
        return pl.ds(pl.multiple_of(down * BY + 8 * g, 8), 8)

    return rows_of, pl.ds(pl.multiple_of(over // 4 * 128, 128), 128), over % 4


def bricks_kernel(
    tissue_ref, estimate_ref, moments_ref, w1_ref, w2_ref, w3_ref, b3_ref,
    out_ref, listing, stack, hidden, partial, result,
):
    means = moments_ref[:, 0:1]
    centre = jnp.sum(means, axis=0, keepdims=True) / DEVICES
    deviation = jnp.sum(moments_ref[:, 1:2] + LOCAL * (means - centre) ** 2, axis=0, keepdims=True)
    spread = jnp.sqrt(deviation / COUNT + 1e-06)
    out_ref[...] = estimate_ref[...]
    many = note_bricks(tissue_ref, listing)
    lane = iota((8, 128), 1)
    row = iota((8, 128), 0)
    group = lane // BX
    column = lane % BX
    tall_group = iota((3 * CH, 128), 1) // BX

    tall_row = iota((TALL, 128), 0)
    tall_column = iota((TALL, 128), 1) % BX
    fixed = (tall_row == 45) | (tall_row == 46)
    fixed |= (tall_row == 47) & (tall_column == 0)
    fixed |= (tall_row == 48) & (tall_column == BX - 1)
    fixed = jnp.where(fixed, 1.0, 0.0)

    @pl.when(many > 0)
    def _():
        @pl.loop(0, SZ * 8)
        def _(k):
            stack[pl.ds(pl.multiple_of(k * TALL, TALL), TALL), :] = fixed

    @pl.loop(0, many)
    def _(n):
        rows_of, lanes, quarter = place_of(listing[n])

        for z in range(SZ):
            plane = jnp.zeros((8, 128), F32)
            for g in range(4):
                block = estimate_ref[z, rows_of(g), lanes]
                turned = pltpu.roll(block, (BX * (g - quarter)) % 128, axis=1)
                plane = jnp.where(group == g, turned, plane)
            plane = (plane - centre) / spread
            before = pltpu.roll(plane, 1, axis=0)
            after = pltpu.roll(plane, 7, axis=0)
            wrapped_before = jnp.where(group == 0, 0.0, pltpu.roll(before, BX, axis=1))
            wrapped_after = jnp.where(group == 3, 0.0, pltpu.roll(after, 128 - BX, axis=1))
            versions = (
                jnp.where(row == 0, wrapped_before, before),
                plane,
                jnp.where(row == 7, wrapped_after, after),
            )
            for b, version in enumerate(versions):
                for c in range(-2, 3):
                    moved = version
                    if c != 0:
                        moved = pltpu.roll(version, -c % 128, axis=1)
                        inside = (column + c >= 0) & (column + c < BX)
                        moved = jnp.where(inside, moved, 0.0)
                    for a in range(3):
                        to = z - (a - 1)
                        if 0 <= to < SZ:
                            at = to * 8 * TALL + 15 * a + 5 * b + c + 2
                            stack[pl.ds(at, 8, stride=TALL), :] = moved

        for z in range(SZ):
            for pair in range(4):
                at = (z * 8 + 2 * pair) * TALL
                taps = [
                    stack[at + TALL * e : at + TALL * (e + 1), :].astype(BF16) for e in range(2)
                ]
                first = jnp.dot(
                    w1_ref[...], jnp.concatenate(taps, axis=1), preferred_element_type=F32
                )
                first = jnp.maximum(first, 0.0)
                for e in range(2):
                    r = 2 * pair + e
                    value = first[:, 128 * e : 128 * (e + 1)]
                    hidden[z, r + 1] = value.astype(BF16)
                    if r == 7:
                        turned = pltpu.roll(value, BX, axis=1)
                        hidden[z, 0] = jnp.where(tall_group == 0, 0.0, turned).astype(BF16)
                    if r == 0:
                        turned = pltpu.roll(value, 128 - BX, axis=1)
                        hidden[z, 9] = jnp.where(tall_group == 3, 0.0, turned).astype(BF16)

        ones = jnp.ones((16, 256), BF16)
        for z in range(SZ):
            for pair in range(4):
                taps = [
                    hidden[z, 2 * pair + e : 2 * pair + e + 3].reshape(9 * CH, 128) for e in range(2)
                ]
                taps = jnp.concatenate([jnp.concatenate(taps, axis=1), ones], axis=0)
                partial[z, pair] = jnp.dot(w2_ref[...], taps, preferred_element_type=F32)

        for z in range(SZ):
            for pair in range(4):
                total = partial[z, pair, CH : 2 * CH]
                if z > 0:
                    total += partial[z - 1, pair, :CH]
                if z < SZ - 1:
                    total += partial[z + 1, pair, 2 * CH :]
                second = jnp.maximum(total, 0.0).astype(BF16)
                last = jnp.dot(w3_ref[...], second, preferred_element_type=F32)
                result[z, 2 * pair : 2 * pair + 1, :] = last[0:1, :128]
                result[z, 2 * pair + 1 : 2 * pair + 2, :] = last[0:1, 128:]

        for z in range(SZ):
            change = (result[z] + b3_ref[...]) * spread
            for g in range(4):
                turned = pltpu.roll(change, (BX * (quarter - g)) % 128, axis=1)
                out_ref[z, rows_of(g), lanes] += jnp.where(group == quarter, turned, 0.0)


def block_weights(w_first, b_first, w_mid, b_mid, w_last):
    taps = w_first.reshape(CH, 9, 3)
    closed = jnp.full((CH,), -1e30, BF16)
    open_ = jnp.zeros((CH,), BF16)
    parts = []

    def two(value):
        high = lax.reduce_precision(value, 8, 7)
        return high.astype(BF16), (value - high).astype(BF16)

    high, rest = two(b_first)
    for c in range(3):
        spread_taps = jnp.pad(taps, ((0, 0), (0, 0), (c, 2 - c))).reshape(CH, 45)
        ends = [high, rest, closed if c == 0 else open_, closed if c == 2 else open_]
        parts.append(jnp.concatenate([spread_taps, jnp.stack(ends, axis=1)], axis=1))
    w1 = jnp.pad(jnp.concatenate(parts, axis=0), ((0, 0), (0, TALL - 49)))
    w2 = w_mid.reshape(3, 9, CH, CH).transpose(0, 2, 1, 3).reshape(3 * CH, 9 * CH)
    high, rest = two(b_mid)
    bias = jnp.pad(jnp.stack([high, rest], axis=1), ((CH, CH), (0, 14)))
    w2 = jnp.concatenate([w2, bias], axis=1)
    w3 = jnp.pad(w_last[None, :], ((0, 15), (0, 0)))
    return w1, w2, w3


def body(observed, psf_taps, psf_index, tissue, w_first, b_first, w_mid, b_mid, w_last, b_last):
    slabs = NZ // SZ
    first_pairs = [(i, i ^ 1) for i in range(slabs)]
    second_pairs = [(i, ((i + 1) ^ 1) - 1) for i in range(1, slabs - 1)]
    swap = [(0, 1), (1, 0)]
    volume = shape((SZ, SY, NX), F32)
    planes = shape((R, SY, NX), BF16)

    def beside(first, second):
        return lax.ppermute(first, "gz", first_pairs), lax.ppermute(second, "gz", second_pairs)

    wide = shape((SZ, SY, WIDE), F32)
    first, second, edge = call(
        prepare_kernel, [planes, planes, shape((SZ, HALO, WIDE), F32)], [observed], [VMEM], limit=8
    )
    first, second = beside(first, second)
    observed_edge = lax.ppermute(edge, "gy", swap)

    normed = psf_taps.transpose(1, 0, 2)
    normed = normed / jnp.sum(normed, axis=2, keepdims=True)
    table, rows_f, rows_a, cols_f, cols_a, inverse, shifted = call(
        setup_kernel,
        [
            shape((2 * SZ * SPAN,), F32),
            shape((SZ, EXT, 256), BF16),
            shape((SZ, SY, 256), BF16),
            shape((SZ, 256, 256), BF16),
            shape((SZ, 256, 256), BF16),
            volume,
            wide,
        ],
        [
            normed.reshape(-1), psf_index,
            jnp.pad(normed.reshape(3 * MODELS, TAPS), ((0, 0), (0, 128 - TAPS))), observed,
        ],
        [SMEM, SMEM, VMEM, VMEM],
        out_specs=[SMEM] + [VMEM] * 6,
        scratch=[
            pltpu.VMEM((128, 128), F32), pltpu.VMEM((128, 128), F32), pltpu.VMEM((128, NX), F32)
        ],
        flops=100_000_000,
        limit=24,
    )

    estimate = observed
    for turn in range(2):
        u, u_edge = call(
            forward_planes_kernel,
            [volume, shape((SZ, HALO, NX), BF16)],
            [table, estimate, first, second, inverse],
            [SMEM] + [VMEM] * 4,
            flops=30 * SZ * SY * NX,
        )
        u_edge = lax.ppermute(u_edge, "gy", swap)
        q, first, second = call(
            ratio_kernel,
            [volume, planes, planes],
            [u, u_edge, shifted, observed_edge, rows_f, rows_a, cols_f, cols_a],
            [VMEM] * 8,
            scratch=[pltpu.VMEM((SZ, EXT, NX), F32), pltpu.VMEM((SZ, EXT, WIDE), F32)],
            flops=1_000_000_000,
            limit=24,
        )
        first, second = beside(first, second)
        ins = [table, q, first, second, estimate, inverse]
        specs = [SMEM] + [VMEM] * 5
        if turn == 0:
            estimate, first, second = call(
                update_kernel, [volume, planes, planes], ins, specs, flops=30 * SZ * SY * NX
            )
            first, second = beside(first, second)
        else:
            estimate, own_moments = call(
                last_update_kernel,
                [volume, shape((DEVICES, 128), F32)],
                ins,
                specs,
                flops=30 * SZ * SY * NX,
            )
    moments = lax.all_to_all(own_moments, ("gz", "gy"), 0, 0, tiled=True)

    w1, w2, w3 = block_weights(w_first, b_first, w_mid, b_mid, w_last)
    (restored,) = call(
        bricks_kernel,
        [volume],
        [tissue.reshape(-1), estimate, moments, w1, w2, w3, b_last[:, None]],
        [SMEM] + [VMEM] * 6,
        scratch=[
            pltpu.SMEM((64,), jnp.int32),
            pltpu.VMEM((SZ * 8 * TALL, 128), F32),
            pltpu.VMEM((SZ, 10, 3 * CH, 128), BF16),
            pltpu.VMEM((SZ, 4, 3 * CH, 256), F32),
            pltpu.VMEM((SZ, 8, 128), F32),
        ],
        flops=1_000_000_000,
        limit=24,
    )
    return restored


def solution(mesh):
    return jax.shard_map(
        body,
        mesh=mesh,
        in_specs=(P("gz", "gy", None), P(), P(), P("gz", "gy", None), P(), P(), P(), P(), P(), P()),
        out_specs=P("gz", "gy", None),
        check_vma=False,
    )
```

```python
import jax
import jax.numpy as jnp
from jax import lax
from jax.experimental import pallas as pl
from jax.experimental.pallas import tpu as pltpu
from jax.sharding import PartitionSpec as P

F32 = jnp.float32
BF16 = jnp.bfloat16
SZ, SY, NX = 8, 64, 512
NZ, NY = 512, 128
TAPS, R = 15, 7
HALO = 16
EXT = SY + HALO
MODELS = 8
BY, BX = 32, 32
CH = 32
ACROSS = NX // BX
BRICKS = (SY // BY) * ACROSS
TALL = 64
DEEP = 9 * CH + 16
WIDE = NX + 128
SPAN = SZ + 2 * R
COUNT = float(NZ * NY * NX)
LOCAL = float(SZ * SY * NX)
DEVICES = 128
AT_FORWARD = 0
AT_ADJOINT = SZ * SPAN
MIB = 1024 * 1024

VMEM = pl.BlockSpec(memory_space=pltpu.VMEM)
SMEM = pl.BlockSpec(memory_space=pltpu.SMEM)


def iota(shape, axis):
    return lax.broadcasted_iota(jnp.int32, shape, axis)


def call(kernel, outs, ins, specs, out_specs=None, scratch=(), flops=0, limit=24):
    moved = sum(x.size * x.dtype.itemsize for x in list(ins) + list(outs))
    return pl.pallas_call(
        kernel,
        out_shape=outs,
        in_specs=specs,
        out_specs=out_specs or [VMEM] * len(outs),
        scratch_shapes=scratch,
        compiler_params=pltpu.CompilerParams(vmem_limit_bytes=limit * MIB),
        cost_estimate=pl.CostEstimate(flops=flops, bytes_accessed=moved, transcendentals=0),
    )(*ins)


def shape(dims, dtype):
    return jax.ShapeDtypeStruct(dims, dtype)


def send_planes(volume_ref, first_ref, second_ref):
    even = 1 - lax.axis_index("gz") % 2

    @pl.loop(0, R)
    def _(k):
        first_ref[k] = volume_ref[k + even].astype(BF16)
        second_ref[k] = volume_ref[k + 1 - even].astype(BF16)


def edge_rows(volume, rows, gy):
    start = pl.multiple_of((1 - gy) * (SY - rows), rows)
    return volume[:, pl.ds(start, rows), :]


def shift_columns(plane):
    left = iota((plane.shape[0], 128), 1) < 64
    turned = pltpu.roll(plane, 64, axis=1)
    edge = turned[:, :128]
    return jnp.concatenate(
        [jnp.where(left, 0.0, edge), turned[:, 128:], jnp.where(left, edge, 0.0)], axis=1
    )


def prepare_kernel(observed_ref, first_ref, second_ref, edge_ref):
    gy = lax.axis_index("gy")
    send_planes(observed_ref, first_ref, second_ref)
    edge = edge_rows(observed_ref, HALO, gy)
    for z in range(SZ):
        edge_ref[z] = shift_columns(edge[z])


def split(value):
    high = value.astype(BF16)
    return high, (value - high.astype(F32)).astype(BF16)


def setup_kernel(
    taps_ref, index_ref, rows_ref, observed_ref,
    table_ref, rows_f_ref, rows_a_ref, cols_f_ref, cols_a_ref, shifted_ref, picked_y, picked_x,
):
    gy = lax.axis_index("gy")
    base = lax.axis_index("gz") * SZ - R

    def model(j):
        plane = base + j
        valid = (plane >= 0) & (plane < NZ)
        return index_ref[jnp.clip(plane, 0, NZ - 1)], valid

    picked_y[...] = jnp.zeros(picked_y.shape, F32)
    picked_x[...] = jnp.zeros(picked_x.shape, F32)
    for j in range(SPAN):
        which, valid = model(j)
        keep = jnp.where(valid, 1.0, 0.0)
        picked_y[j : j + 1, :] = rows_ref[pl.ds(MODELS + which, 1), :] * keep
        picked_x[j : j + 1, :] = rows_ref[pl.ds(2 * MODELS + which, 1), :] * keep
        for z in range(SZ):
            if 0 <= j - z < TAPS:
                own, _ = model(z + R)
                table_ref[AT_FORWARD + z * SPAN + j] = taps_ref[own * TAPS + j - z] * keep
                table_ref[AT_ADJOINT + j * SZ + z] = (
                    taps_ref[which * TAPS + z + TAPS - 1 - j] * keep
                )

    def place(index):
        return jnp.where(index < SY, index, jnp.where(gy == 0, index, index - EXT))

    lane = iota((EXT, 256), 1)
    piece = lane // EXT
    inside = place(lane - piece * EXT)
    outside = place(iota((EXT, 256), 0))
    used = piece < 3
    tap_f = jnp.where(used, inside - outside + R, -1)
    tap_a = jnp.where(used, outside - inside + R, -1)[:SY]
    low = piece == 1
    source = iota((256, 128), 0)
    target = iota((256, 128), 1)
    tap_cf = source - target - (64 - R)
    tap_ca = target - source + (64 + R)

    @pl.loop(0, SZ)
    def _(z):
        own, _ = model(z + R)

        def table(taps, axis):
            at = (axis * MODELS + own) * TAPS
            total = jnp.zeros(taps.shape, F32)
            for t in range(TAPS):
                total = jnp.where(taps == t, taps_ref[at + t], total)
            return total

        def halves(value, is_low):
            high = value.astype(BF16).astype(F32)
            return jnp.where(is_low, value - high, high).astype(BF16)

        rows_f_ref[z] = halves(table(tap_f, 1), low)
        rows_a_ref[z] = halves(table(tap_a, 1), low[:SY])
        for taps, out in ((tap_cf, cols_f_ref), (tap_ca, cols_a_ref)):
            high, rest = split(table(taps, 2))
            out[z, :, :128] = high
            out[z, :, 128:] = rest
        shifted_ref[z] = shift_columns(observed_ref[z])

def exact(left, right, contract):
    return lax.dot_general(
        left, right, (contract, ((), ())),
        precision=lax.Precision.HIGHEST, preferred_element_type=F32,
    )


def column_of(row):
    same = iota((CH, CH), 0) == iota((CH, CH), 1)
    return jnp.sum(jnp.where(same, row, 0.0), axis=1, keepdims=True)


def second_setup_kernel(
    table_ref, picked_y_ref, picked_x_ref, w_first_ref, b_first_ref, w_mid_ref, b_mid_ref, after_ref,
    inverse_ref, w1_ref, w2_ref, scaled,
):
    del after_ref
    gy = lax.axis_index("gy")
    at_y = iota((SY, 128), 0) + gy * SY + R - iota((SY, 128), 1)
    at_x = iota((128, NX), 1) + R - iota((128, NX), 0)
    along = exact(
        jnp.where((at_y >= 0) & (at_y < NY), 1.0, 0.0), picked_y_ref[...], ((1,), (1,))
    )
    across = exact(picked_x_ref[...], jnp.where((at_x >= 0) & (at_x < NX), 1.0, 0.0), ((1,), (0,)))
    for z in range(SZ):
        scaled[...] = jnp.zeros(scaled.shape, F32)
        for j in range(z, z + TAPS):
            scaled[j : j + 1, :] = across[j : j + 1, :] * table_ref[AT_ADJOINT + j * SZ + z]
        inverse_ref[z] = 1.0 / exact(along, scaled[...], ((1,), (0,)))

    tap = iota((27, TALL), 0)
    at = iota((27, TALL), 1)
    lane = iota((CH, TALL), 1)
    high, rest = split(column_of(b_first_ref[...]))
    ends = jnp.where(lane == 45, high.astype(F32), 0.0) + jnp.where(lane == 46, rest.astype(F32), 0.0)
    for c in range(3):
        moved = (at == 5 * (tap // 3) + tap % 3 + c).astype(BF16)
        block = jnp.dot(w_first_ref[...], moved, preferred_element_type=F32) + ends
        if c != 1:
            block += jnp.where(lane == (47 if c == 0 else 48), -1e30, 0.0)
        w1_ref[CH * c : CH * (c + 1), :] = block.astype(BF16)

    lane = iota((CH, DEEP), 1)
    channel = iota((CH, DEEP), 0)
    high, rest = split(column_of(b_mid_ref[...]))
    ends = jnp.where(lane == 9 * CH, high.astype(F32), 0.0)
    ends += jnp.where(lane == 9 * CH + 1, rest.astype(F32), 0.0)
    for a in range(3):
        block = ends if a == 1 else jnp.zeros((CH, DEEP), F32)
        for t in range(9):
            moved = (lane == CH * t + channel).astype(BF16)
            block += jnp.dot(w_mid_ref[9 * a + t], moved, preferred_element_type=F32)
        w2_ref[CH * a : CH * (a + 1), :] = block.astype(BF16)


def plane_pass(coefficient, own_ref, first_ref, second_ref, emit):
    even = lax.axis_index("gz") % 2 == 0
    high, wide = 16, 256

    def run(low_ref, high_ref):
        @pl.loop(0, SY // high)
        def _(block):
            rows = pl.ds(pl.multiple_of(block * high, high), high)
            for part in range(NX // wide):
                lanes = pl.ds(part * wide, wide)
                planes = [low_ref[k, rows, lanes].astype(F32) for k in range(R)]
                planes += [own_ref[k, rows, lanes] for k in range(SZ)]
                planes += [high_ref[k, rows, lanes].astype(F32) for k in range(R)]
                for z in range(SZ):
                    terms = [coefficient(z, j) * planes[j] for j in range(z, z + TAPS)]
                    while len(terms) > 1:
                        terms = [sum(terms[i : i + 2]) for i in range(0, len(terms), 2)]
                    emit(z, rows, lanes, terms[0])

    @pl.when(even)
    def _():
        run(second_ref, first_ref)

    @pl.when(jnp.logical_not(even))
    def _():
        run(first_ref, second_ref)


def forward_planes_kernel(table_ref, own_ref, first_ref, second_ref, out_ref, edge_ref):
    def emit(z, rows, lanes, value):
        out_ref[z, rows, lanes] = value

    plane_pass(
        lambda z, j: table_ref[AT_FORWARD + z * SPAN + j], own_ref, first_ref, second_ref, emit
    )
    edge_ref[...] = edge_rows(out_ref, HALO, lax.axis_index("gy")).astype(BF16)


def adjoint_coefficient(table_ref):
    return lambda z, j: table_ref[AT_ADJOINT + j * SZ + z]


def update_kernel(
    table_ref, own_ref, first_ref, second_ref, before_ref, inverse_ref, out_ref, to_first_ref, to_second_ref
):
    def emit(z, rows, lanes, value):
        out_ref[z, rows, lanes] = (
            before_ref[z, rows, lanes] * value * inverse_ref[z, rows, lanes]
        )

    plane_pass(adjoint_coefficient(table_ref), own_ref, first_ref, second_ref, emit)
    send_planes(out_ref, to_first_ref, to_second_ref)


def last_update_kernel(
    table_ref, own_ref, first_ref, second_ref, before_ref, inverse_ref, out_ref, moments_ref
):
    def emit(z, rows, lanes, value):
        out_ref[z, rows, lanes] = (
            before_ref[z, rows, lanes] * value * inverse_ref[z, rows, lanes]
        )

    plane_pass(adjoint_coefficient(table_ref), own_ref, first_ref, second_ref, emit)
    total = jnp.zeros((SY, NX), F32)
    for z in range(SZ):
        total += out_ref[z]
    mean = jnp.sum(total, keepdims=True) / LOCAL
    squares = jnp.zeros((SY, NX), F32)
    for z in range(SZ):
        squares += (out_ref[z] - mean) ** 2
    deviation = jnp.sum(squares, keepdims=True)
    moments_ref[...] = jnp.where(iota((DEVICES, 128), 1) == 0, mean, deviation)


def windows_of(blocks):
    blocks = [b.astype(BF16) for b in blocks]
    pairs = [jnp.concatenate(blocks[j : j + 2], axis=1) for j in range(len(blocks) - 1)]
    return jnp.concatenate(pairs, axis=0)


def column_pass(blocks, matrix):
    product = jnp.dot(windows_of(blocks), matrix, preferred_element_type=F32)
    product = product[:, :128] + product[:, 128:]
    return [product[EXT * j : EXT * (j + 1)] for j in range(len(blocks) - 1)]


def row_pass(matrix, value):
    high, rest = split(value)
    stacked = jnp.concatenate([high, high, rest, jnp.zeros((16, NX), BF16)], axis=0)
    return jnp.dot(matrix, stacked, preferred_element_type=F32)


def ratio_kernel(
    u_ref, u_edge_ref, observed_ref, observed_edge_ref,
    rows_f_ref, rows_a_ref, cols_f_ref, cols_a_ref,
    out_ref, to_first_ref, to_second_ref,
    wide, wider,
):
    columns = NX // 128
    left = iota((EXT, 128), 1) < 64
    none = jnp.zeros((EXT, 128), F32)
    for z in range(SZ):
        extended = jnp.concatenate([u_ref[z], u_edge_ref[z].astype(F32)], axis=0)
        wide[z] = row_pass(rows_f_ref[z], extended)
    for z in range(SZ):
        blocks = [wide[z, :, 128 * j : 128 * (j + 1)] for j in range(columns)]
        blurred = column_pass([none] + blocks + [none], cols_f_ref[z])
        blurred[0] = jnp.where(left, 1.0, blurred[0])
        blurred[-1] = jnp.where(left, blurred[-1], 1.0)
        for j, block in enumerate(blurred):
            lanes = slice(128 * j, 128 * (j + 1))
            wider[z, :SY, lanes] = observed_ref[z, :, lanes] / block[:SY]
            wider[z, SY:, lanes] = observed_edge_ref[z, :, lanes] / block[SY:]
    for z in range(SZ):
        blocks = [wider[z, :, 128 * j : 128 * (j + 1)] for j in range(columns + 1)]
        wide[z] = jnp.concatenate(column_pass(blocks, cols_a_ref[z]), axis=1)
    for z in range(SZ):
        out_ref[z] = row_pass(rows_a_ref[z], wide[z])
    send_planes(out_ref, to_first_ref, to_second_ref)


def note_bricks(tissue_ref, listing):
    def note(b, count):
        listing[count] = b
        return count + jnp.where(tissue_ref[0, b // ACROSS, b % ACROSS] > 0, 1, 0)

    return lax.fori_loop(0, BRICKS, note, 0)


def place_of(brick):
    down = brick // ACROSS
    over = brick % ACROSS

    def rows_of(g):
        return pl.ds(pl.multiple_of(down * BY + 8 * g, 8), 8)

    return rows_of, pl.ds(pl.multiple_of(over // 4 * 128, 128), 128), over % 4


def bricks_kernel(
    tissue_ref, estimate_ref, moments_ref, w1_ref, w2_ref, w3_ref, b3_ref,
    out_ref, listing, stack, hidden, partial, result,
):
    means = moments_ref[:, 0:1]
    centre = jnp.sum(means, axis=0, keepdims=True) / DEVICES
    deviation = jnp.sum(moments_ref[:, 1:2] + LOCAL * (means - centre) ** 2, axis=0, keepdims=True)
    spread = jnp.sqrt(deviation / COUNT + 1e-06)
    out_ref[...] = estimate_ref[...]
    many = note_bricks(tissue_ref, listing)
    lane = iota((8, 128), 1)
    row = iota((8, 128), 0)
    group = lane // BX
    column = lane % BX
    tall_group = iota((3 * CH, 128), 1) // BX

    tall_row = iota((TALL, 128), 0)
    tall_column = iota((TALL, 128), 1) % BX
    fixed = (tall_row == 45) | (tall_row == 46)
    fixed |= (tall_row == 47) & (tall_column == 0)
    fixed |= (tall_row == 48) & (tall_column == BX - 1)
    fixed = jnp.where(fixed, 1.0, 0.0)

    @pl.when(many > 0)
    def _():
        @pl.loop(0, SZ * 8)
        def _(k):
            stack[pl.ds(pl.multiple_of(k * TALL, TALL), TALL), :] = fixed

    @pl.loop(0, many)
    def _(n):
        rows_of, lanes, quarter = place_of(listing[n])

        for z in range(SZ):
            plane = jnp.zeros((8, 128), F32)
            for g in range(4):
                block = estimate_ref[z, rows_of(g), lanes]
                turned = pltpu.roll(block, (BX * (g - quarter)) % 128, axis=1)
                plane = jnp.where(group == g, turned, plane)
            plane = (plane - centre) / spread
            before = pltpu.roll(plane, 1, axis=0)
            after = pltpu.roll(plane, 7, axis=0)
            wrapped_before = jnp.where(group == 0, 0.0, pltpu.roll(before, BX, axis=1))
            wrapped_after = jnp.where(group == 3, 0.0, pltpu.roll(after, 128 - BX, axis=1))
            versions = (
                jnp.where(row == 0, wrapped_before, before),
                plane,
                jnp.where(row == 7, wrapped_after, after),
            )
            for b, version in enumerate(versions):
                for c in range(-2, 3):
                    moved = version
                    if c != 0:
                        moved = pltpu.roll(version, -c % 128, axis=1)
                        inside = (column + c >= 0) & (column + c < BX)
                        moved = jnp.where(inside, moved, 0.0)
                    for a in range(3):
                        to = z - (a - 1)
                        if 0 <= to < SZ:
                            at = to * 8 * TALL + 15 * a + 5 * b + c + 2
                            stack[pl.ds(at, 8, stride=TALL), :] = moved

        for z in range(SZ):
            for pair in range(4):
                at = (z * 8 + 2 * pair) * TALL
                taps = [
                    stack[at + TALL * e : at + TALL * (e + 1), :].astype(BF16) for e in range(2)
                ]
                first = jnp.dot(
                    w1_ref[...], jnp.concatenate(taps, axis=1), preferred_element_type=F32
                )
                first = jnp.maximum(first, 0.0)
                for e in range(2):
                    r = 2 * pair + e
                    value = first[:, 128 * e : 128 * (e + 1)]
                    hidden[z, r + 1] = value.astype(BF16)
                    if r == 7:
                        turned = pltpu.roll(value, BX, axis=1)
                        hidden[z, 0] = jnp.where(tall_group == 0, 0.0, turned).astype(BF16)
                    if r == 0:
                        turned = pltpu.roll(value, 128 - BX, axis=1)
                        hidden[z, 9] = jnp.where(tall_group == 3, 0.0, turned).astype(BF16)

        ones = jnp.ones((DEEP - 9 * CH, 256), BF16)
        last_weights = jnp.broadcast_to(w3_ref[...].astype(F32), (16, CH)).astype(BF16)
        for z in range(SZ):
            for pair in range(4):
                taps = [
                    hidden[z, 2 * pair + e : 2 * pair + e + 3].reshape(9 * CH, 128) for e in range(2)
                ]
                taps = jnp.concatenate([jnp.concatenate(taps, axis=1), ones], axis=0)
                partial[z, pair] = jnp.dot(w2_ref[...], taps, preferred_element_type=F32)

        for z in range(SZ):
            for pair in range(4):
                total = partial[z, pair, CH : 2 * CH]
                if z > 0:
                    total += partial[z - 1, pair, :CH]
                if z < SZ - 1:
                    total += partial[z + 1, pair, 2 * CH :]
                second = jnp.maximum(total, 0.0).astype(BF16)
                last = jnp.dot(last_weights, second, preferred_element_type=F32)
                result[z, 2 * pair : 2 * pair + 1, :] = last[0:1, :128]
                result[z, 2 * pair + 1 : 2 * pair + 2, :] = last[0:1, 128:]

        for z in range(SZ):
            change = (result[z] + b3_ref[0]) * spread
            for g in range(4):
                turned = pltpu.roll(change, (BX * (quarter - g)) % 128, axis=1)
                out_ref[z, rows_of(g), lanes] += jnp.where(group == quarter, turned, 0.0)


def body(observed, psf_taps, psf_index, tissue, w_first, b_first, w_mid, b_mid, w_last, b_last):
    slabs = NZ // SZ
    first_pairs = [(i, i ^ 1) for i in range(slabs)]
    second_pairs = [(i, ((((i + 1) % slabs) ^ 1) - 1) % slabs) for i in range(slabs)]
    swap = [(0, 1), (1, 0)]
    volume = shape((SZ, SY, NX), F32)
    planes = shape((R, SY, NX), BF16)

    def beside(first, second):
        return lax.ppermute(first, "gz", first_pairs), lax.ppermute(second, "gz", second_pairs)

    wide = shape((SZ, SY, WIDE), F32)
    first, second, edge = call(
        prepare_kernel, [planes, planes, shape((SZ, HALO, WIDE), F32)], [observed], [VMEM], limit=8
    )
    first, second = beside(first, second)
    observed_edge = lax.ppermute(edge, "gy", swap)

    normed = psf_taps.transpose(1, 0, 2)
    normed = normed / jnp.sum(normed, axis=2, keepdims=True)
    table, rows_f, rows_a, cols_f, cols_a, shifted, picked_y, picked_x = call(
        setup_kernel,
        [
            shape((2 * SZ * SPAN,), F32),
            shape((SZ, EXT, 256), BF16),
            shape((SZ, SY, 256), BF16),
            shape((SZ, 256, 256), BF16),
            shape((SZ, 256, 256), BF16),
            wide,
            shape((128, 128), F32),
            shape((128, 128), F32),
        ],
        [
            normed.reshape(-1), psf_index,
            jnp.pad(normed.reshape(3 * MODELS, TAPS), ((0, 0), (0, 128 - TAPS))), observed,
        ],
        [SMEM, SMEM, VMEM, VMEM],
        out_specs=[SMEM] + [VMEM] * 7,
        flops=100_000_000,
        limit=24,
    )

    estimate = observed
    for turn in range(2):
        u, u_edge = call(
            forward_planes_kernel,
            [volume, shape((SZ, HALO, NX), BF16)],
            [table, estimate, first, second],
            [SMEM] + [VMEM] * 3,
            flops=30 * SZ * SY * NX,
        )
        u_edge = lax.ppermute(u_edge, "gy", swap)
        q, first, second = call(
            ratio_kernel,
            [volume, planes, planes],
            [u, u_edge, shifted, observed_edge, rows_f, rows_a, cols_f, cols_a],
            [VMEM] * 8,
            scratch=[pltpu.VMEM((SZ, EXT, NX), F32), pltpu.VMEM((SZ, EXT, WIDE), F32)],
            flops=1_000_000_000,
            limit=24,
        )
        first, second = beside(first, second)
        if turn == 0:
            inverse, w1, w2 = call(
                second_setup_kernel,
                [volume, shape((3 * CH, TALL), BF16), shape((3 * CH, DEEP), BF16)],
                [
                    table, picked_y, picked_x, w_first, b_first[None], w_mid, b_mid[None], q,
                ],
                [SMEM] + [VMEM] * 6 + [pl.BlockSpec(memory_space=pl.ANY)],
                scratch=[pltpu.VMEM((128, NX), F32)],
                flops=100_000_000,
            )
        ins = [table, q, first, second, estimate, inverse]
        specs = [SMEM] + [VMEM] * 5
        if turn == 0:
            estimate, first, second = call(
                update_kernel, [volume, planes, planes], ins, specs, flops=30 * SZ * SY * NX
            )
            first, second = beside(first, second)
        else:
            estimate, own_moments = call(
                last_update_kernel,
                [volume, shape((DEVICES, 128), F32)],
                ins,
                specs,
                flops=30 * SZ * SY * NX,
            )
    moments = lax.all_to_all(own_moments, ("gz", "gy"), 0, 0, tiled=True)

    (restored,) = call(
        bricks_kernel,
        [volume],
        [tissue, estimate, moments, w1, w2, w_last[None], b_last],
        [SMEM] + [VMEM] * 5 + [SMEM],
        scratch=[
            pltpu.SMEM((64,), jnp.int32),
            pltpu.VMEM((SZ * 8 * TALL, 128), F32),
            pltpu.VMEM((SZ, 10, 3 * CH, 128), BF16),
            pltpu.VMEM((SZ, 4, 3 * CH, 256), F32),
            pltpu.VMEM((SZ, 8, 128), F32),
        ],
        flops=1_000_000_000,
        limit=24,
    )
    return restored


def solution(mesh):
    return jax.shard_map(
        body,
        mesh=mesh,
        in_specs=(P("gz", "gy", None), P(), P(), P("gz", "gy", None), P(), P(), P(), P(), P(), P()),
        out_specs=P("gz", "gy", None),
        check_vma=False,
    )
```

```python
import functools

import jax
import jax.numpy as jnp
from jax import lax
from jax.experimental import pallas as pl
from jax.experimental.pallas import tpu as pltpu
from jax.sharding import PartitionSpec as P

F32 = jnp.float32
BF16 = jnp.bfloat16
SZ, SY, NX = 8, 64, 512
NZ, NY = 512, 128
TAPS, R = 15, 7
HALO = 16
EXT = SY + HALO
MODELS = 8
BY, BX = 32, 32
CH = 32
ACROSS = NX // BX
BRICKS = (SY // BY) * ACROSS
MOST = 3
FLAT = 16
STACK = 3 * FLAT
TALL = 64
DEEP = 9 * CH + 16
WIDE = NX + 128
SPAN = SZ + 2 * R
ROWS = 24
COUNT = float(NZ * NY * NX)
LOCAL = float(SZ * SY * NX)
DEVICES = 128
MIB = 1024 * 1024

VMEM = pl.BlockSpec(memory_space=pltpu.VMEM)
SMEM = pl.BlockSpec(memory_space=pltpu.SMEM)


def iota(shape, axis):
    return lax.broadcasted_iota(jnp.int32, shape, axis)


def call(kernel, outs, ins, specs, out_specs=None, scratch=(), flops=0, limit=24):
    moved = sum(x.size * x.dtype.itemsize for x in list(ins) + list(outs))
    return pl.pallas_call(
        kernel,
        out_shape=outs,
        in_specs=specs,
        out_specs=out_specs or [VMEM] * len(outs),
        scratch_shapes=scratch,
        compiler_params=pltpu.CompilerParams(vmem_limit_bytes=limit * MIB),
        cost_estimate=pl.CostEstimate(flops=flops, bytes_accessed=moved, transcendentals=0),
    )(*ins)


def shape(dims, dtype):
    return jax.ShapeDtypeStruct(dims, dtype)


def send_planes(volume_ref, first_ref, second_ref):
    even = 1 - lax.axis_index("gz") % 2

    @pl.loop(0, R)
    def _(k):
        first_ref[k] = volume_ref[k + even].astype(BF16)
        second_ref[k] = volume_ref[k + 1 - even].astype(BF16)


def edge_rows(volume, rows, gy):
    start = pl.multiple_of((1 - gy) * (SY - rows), rows)
    return volume[:, pl.ds(start, rows), :]


def shift_columns(plane):
    left = iota((plane.shape[0], 128), 1) < 64
    turned = pltpu.roll(plane, 64, axis=1)
    edge = turned[:, :128]
    return jnp.concatenate(
        [jnp.where(left, 0.0, edge), turned[:, 128:], jnp.where(left, edge, 0.0)], axis=1
    )


def prepare_kernel(observed_ref, first_ref, second_ref, edge_ref):
    gy = lax.axis_index("gy")
    send_planes(observed_ref, first_ref, second_ref)
    edge = edge_rows(observed_ref, HALO, gy)
    for z in range(SZ):
        edge_ref[z] = shift_columns(edge[z])


def split(value):
    high = value.astype(BF16)
    return high, (value - high.astype(F32)).astype(BF16)


def setup_kernel(
    taps_ref, index_ref, observed_ref,
    table_ref, rows_f_ref, rows_a_ref, cols_f_ref, cols_a_ref, shifted_ref, picked_y, picked_x,
    rows, picked_z, turned_f, turned_a,
):
    gy = lax.axis_index("gy")
    base = lax.axis_index("gz") * SZ - R

    rows[...] = jnp.zeros(rows.shape, F32)
    for axis in range(3):
        taps = taps_ref[axis]
        total = jnp.sum(taps, axis=1, keepdims=True)
        rows[MODELS * axis : MODELS * (axis + 1), :TAPS] = taps / total
    for picked in (picked_z, picked_y, picked_x):
        picked[...] = jnp.zeros(picked.shape, F32)
    for j in range(SPAN):
        plane = base + j
        keep = jnp.where((plane >= 0) & (plane < NZ), 1.0, 0.0)
        which = index_ref[jnp.clip(plane, 0, NZ - 1)]
        for axis, picked in enumerate((picked_z, picked_y, picked_x)):
            picked[j : j + 1, :] = rows[pl.ds(MODELS * axis + which, 1), :] * keep

    lane = iota((ROWS, 128), 1)
    plane = iota((ROWS, 128), 0)
    valid = (plane + base >= 0) & (plane + base < NZ)
    wanted = [
        jnp.where((lane == plane - z) & valid, picked_z[R + z : R + z + 1, :], 0.0)
        for z in range(SZ)
    ]
    wanted += [
        jnp.where(lane == z + TAPS - 1 - plane, picked_z[:ROWS, :], 0.0) for z in range(SZ)
    ]
    table_ref[...] = exact(
        jnp.concatenate(wanted, axis=0), jnp.ones((128, 128), F32), ((1,), (0,))
    )

    def place(index):
        return jnp.where(index < SY, index, jnp.where(gy == 0, index, index - EXT))

    lane = iota((EXT, 256), 1)
    piece = lane // EXT
    inside = place(lane - piece * EXT)
    outside = place(iota((EXT, 256), 0))
    used = piece < 3
    tap_f = jnp.where(used, inside - outside + R, -1)
    tap_a = jnp.where(used, outside - inside + R, -1)[:SY]
    low = piece == 1
    source = iota((256, 128), 0)
    target = iota((256, 128), 1)
    tap_cf = source - target - (64 - R)
    tap_ca = target - source + (64 + R)
    held_f = (tap_cf >= 0) & (tap_cf < TAPS)
    held_a = (tap_ca >= 0) & (tap_ca < TAPS)
    tap = iota((128, 128), 0)
    to = iota((128, 128), 1)
    columns = picked_x[:ROWS, :]
    turned_f[...] = exact(columns, jnp.where(to == 64 + R - tap, 1.0, 0.0), ((1,), (0,)))
    turned_a[...] = exact(columns, jnp.where(to == 64 - R + tap, 1.0, 0.0), ((1,), (0,)))

    @pl.loop(0, SZ)
    def _(z):
        taps = picked_y[pl.ds(z + R, 1), :]
        taps = [taps[:, t : t + 1] for t in range(TAPS)]

        def table(which):
            total = jnp.zeros(which.shape, F32)
            for t in range(TAPS):
                total = jnp.where(which == t, taps[t], total)
            return total

        def halves(value, is_low):
            high = value.astype(BF16).astype(F32)
            return jnp.where(is_low, value - high, high).astype(BF16)

        rows_f_ref[z] = halves(table(tap_f), low)
        rows_a_ref[z] = halves(table(tap_a), low[:SY])
        for turned, held, out in (
            (turned_f, held_f, cols_f_ref), (turned_a, held_a, cols_a_ref)
        ):
            band = jnp.broadcast_to(turned[pl.ds(z + R, 1), :], (256, 128))
            band = pltpu.roll(band, 0, axis=1, stride=1, stride_axis=0)
            high, rest = split(jnp.where(held, band, 0.0))
            out[z, :, :128] = high
            out[z, :, 128:] = rest
        shifted_ref[z] = shift_columns(observed_ref[z])


def exact(left, right, contract):
    return lax.dot_general(
        left, right, (contract, ((), ())),
        precision=lax.Precision.HIGHEST, preferred_element_type=F32,
    )


def column_of(row):
    same = iota((CH, CH), 0) == iota((CH, CH), 1)
    return jnp.sum(jnp.where(same, row, 0.0), axis=1, keepdims=True)


def second_setup_kernel(
    table_ref, picked_y_ref, picked_x_ref, w_first_ref, b_first_ref, w_mid_ref, b_mid_ref, after_ref,
    inverse_ref, w1_ref, w2_ref, scaled,
):
    del after_ref
    gy = lax.axis_index("gy")
    at_y = iota((SY, 128), 0) + gy * SY + R - iota((SY, 128), 1)
    at_x = iota((128, NX), 1) + R - iota((128, NX), 0)
    along = exact(
        jnp.where((at_y >= 0) & (at_y < NY), 1.0, 0.0), picked_y_ref[...], ((1,), (1,))
    )
    across = exact(picked_x_ref[...], jnp.where((at_x >= 0) & (at_x < NX), 1.0, 0.0), ((1,), (0,)))
    scaled[...] = jnp.zeros(scaled.shape, F32)
    for z in range(SZ):
        weight = table_ref[(SZ + z) * ROWS : (SZ + z + 1) * ROWS, :]
        scaled[:ROWS, :] = across[:ROWS] * jnp.concatenate([weight] * (NX // 128), axis=1)
        inverse_ref[z] = 1.0 / exact(along, scaled[...], ((1,), (0,)))

    tap = iota((27, TALL), 0)
    at = iota((27, TALL), 1)
    lane = iota((CH, TALL), 1)
    high, rest = split(column_of(b_first_ref[...]))
    ends = jnp.where(lane == STACK, high.astype(F32), 0.0) + jnp.where(lane == STACK + 1, rest.astype(F32), 0.0)
    for c in range(3):
        moved = (at == FLAT * (tap // 9) + 5 * (tap // 3 % 3) + tap % 3 + c).astype(BF16)
        block = jnp.dot(w_first_ref[...], moved, preferred_element_type=F32) + ends
        if c != 1:
            block += jnp.where(lane == (STACK + 2 if c == 0 else STACK + 3), -1e30, 0.0)
        w1_ref[CH * c : CH * (c + 1), :] = block.astype(BF16)

    lane = iota((CH, DEEP), 1)
    channel = iota((CH, DEEP), 0)
    high, rest = split(column_of(b_mid_ref[...]))
    ends = jnp.where(lane == 9 * CH, high.astype(F32), 0.0)
    ends += jnp.where(lane == 9 * CH + 1, rest.astype(F32), 0.0)
    for a in range(3):
        block = ends if a == 1 else jnp.zeros((CH, DEEP), F32)
        for t in range(9):
            moved = (lane == CH * t + channel).astype(BF16)
            block += jnp.dot(w_mid_ref[9 * a + t], moved, preferred_element_type=F32)
        w2_ref[CH * a : CH * (a + 1), :] = block.astype(BF16)


def blocks_of(body):
    high = 32

    @pl.loop(0, SY // high)
    def _(block):
        rows = pl.ds(pl.multiple_of(block * high, high), high)
        for part in range(NX // 128):
            body(rows, slice(128 * part, 128 * (part + 1)))


def added(terms):
    while len(terms) > 1:
        terms = [sum(terms[i : i + 2]) for i in range(0, len(terms), 2)]
    return terms[0]


def own_planes_kernel(kind, table_ref, own_ref, out_ref):
    def block(rows, lanes):
        planes = [own_ref[k, rows, lanes] for k in range(SZ)]
        for z in range(SZ):
            at = (kind * SZ + z) * ROWS + R
            out_ref[z, rows, lanes] = added(
                [table_ref[at + k : at + k + 1, :] * planes[k] for k in range(SZ)]
            )

    blocks_of(block)


def plane_pass(kind, table_ref, sum_ref, first_ref, second_ref, emit):
    even = lax.axis_index("gz") % 2 == 0

    def run(low_ref, high_ref):
        def block(rows, lanes):
            low = [low_ref[k, rows, lanes].astype(F32) for k in range(R)]
            high = [high_ref[k, rows, lanes].astype(F32) for k in range(R)]
            for z in range(SZ):
                at = (kind * SZ + z) * ROWS
                terms = [sum_ref[z, rows, lanes]]
                terms += [table_ref[at + k : at + k + 1, :] * low[k] for k in range(z, R)]
                at += R + SZ
                terms += [table_ref[at + k : at + k + 1, :] * high[k] for k in range(z)]
                emit(z, rows, lanes, added(terms))

        blocks_of(block)

    @pl.when(even)
    def _():
        run(second_ref, first_ref)

    @pl.when(jnp.logical_not(even))
    def _():
        run(first_ref, second_ref)


def forward_planes_kernel(table_ref, sum_ref, first_ref, second_ref, out_ref, edge_ref):
    def emit(z, rows, lanes, value):
        out_ref[z, rows, lanes] = value

    plane_pass(0, table_ref, sum_ref, first_ref, second_ref, emit)
    edge_ref[...] = edge_rows(out_ref, HALO, lax.axis_index("gy")).astype(BF16)


def update(table_ref, sum_ref, first_ref, second_ref, before_ref, inverse_ref, out_ref):
    def emit(z, rows, lanes, value):
        out_ref[z, rows, lanes] = (
            before_ref[z, rows, lanes] * value * inverse_ref[z, rows, lanes]
        )

    plane_pass(1, table_ref, sum_ref, first_ref, second_ref, emit)


def update_kernel(
    table_ref, sum_ref, first_ref, second_ref, before_ref, inverse_ref, out_ref, to_first_ref, to_second_ref
):
    update(table_ref, sum_ref, first_ref, second_ref, before_ref, inverse_ref, out_ref)
    send_planes(out_ref, to_first_ref, to_second_ref)


def last_update_kernel(
    table_ref, sum_ref, first_ref, second_ref, before_ref, inverse_ref, out_ref, moments_ref
):
    update(table_ref, sum_ref, first_ref, second_ref, before_ref, inverse_ref, out_ref)
    total = jnp.zeros((SY, NX), F32)
    for z in range(SZ):
        total += out_ref[z]
    mean = jnp.sum(total, keepdims=True) / LOCAL
    squares = jnp.zeros((SY, NX), F32)
    for z in range(SZ):
        squares += (out_ref[z] - mean) ** 2
    deviation = jnp.sum(squares, keepdims=True)
    moments_ref[...] = jnp.where(iota((DEVICES, 128), 1) == 0, mean, deviation)


def windows_of(blocks):
    blocks = [b.astype(BF16) for b in blocks]
    pairs = [jnp.concatenate(blocks[j : j + 2], axis=1) for j in range(len(blocks) - 1)]
    return jnp.concatenate(pairs, axis=0)


def column_pass(blocks, matrix):
    product = jnp.dot(windows_of(blocks), matrix, preferred_element_type=F32)
    product = product[:, :128] + product[:, 128:]
    return [product[EXT * j : EXT * (j + 1)] for j in range(len(blocks) - 1)]


def row_pass(matrix, value):
    high, rest = split(value)
    stacked = jnp.concatenate([high, high, rest, jnp.zeros((16, NX), BF16)], axis=0)
    return jnp.dot(matrix, stacked, preferred_element_type=F32)


def ratio_kernel(
    u_ref, u_edge_ref, observed_ref, observed_edge_ref,
    rows_f_ref, rows_a_ref, cols_f_ref, cols_a_ref,
    out_ref, to_first_ref, to_second_ref,
    wide, wider,
):
    columns = NX // 128
    left = iota((EXT, 128), 1) < 64
    none = jnp.zeros((EXT, 128), F32)
    for z in range(SZ):
        extended = jnp.concatenate([u_ref[z], u_edge_ref[z].astype(F32)], axis=0)
        wide[z] = row_pass(rows_f_ref[z], extended)
    for z in range(SZ):
        blocks = [wide[z, :, 128 * j : 128 * (j + 1)] for j in range(columns)]
        blurred = column_pass([none] + blocks + [none], cols_f_ref[z])
        blurred[0] = jnp.where(left, 1.0, blurred[0])
        blurred[-1] = jnp.where(left, blurred[-1], 1.0)
        for j, block in enumerate(blurred):
            lanes = slice(128 * j, 128 * (j + 1))
            wider[z, :SY, lanes] = observed_ref[z, :, lanes] / block[:SY]
            wider[z, SY:, lanes] = observed_edge_ref[z, :, lanes] / block[SY:]
    for z in range(SZ):
        blocks = [wider[z, :, 128 * j : 128 * (j + 1)] for j in range(columns + 1)]
        wide[z] = jnp.concatenate(column_pass(blocks, cols_a_ref[z]), axis=1)
    for z in range(SZ):
        out_ref[z] = row_pass(rows_a_ref[z], wide[z])
    send_planes(out_ref, to_first_ref, to_second_ref)


def note_bricks(tissue_ref, listing):
    def note(b, count):
        listing[count] = b
        return count + jnp.where(tissue_ref[0, b // ACROSS, b % ACROSS] > 0, 1, 0)

    return lax.fori_loop(0, BRICKS, note, 0)


def place_of(brick):
    down = brick // ACROSS
    over = brick % ACROSS

    def rows_of(g):
        return pl.ds(pl.multiple_of(down * BY + 8 * g, 8), 8)

    return rows_of, pl.ds(pl.multiple_of(over // 4 * 128, 128), 128), over % 4


def stack_kernel(tissue_ref, estimate_ref, out_ref, listing):
    many = note_bricks(tissue_ref, listing)
    lane = iota((8, 128), 1)
    row = iota((8, 128), 0)
    group = lane // BX
    column = lane % BX

    @pl.loop(0, many)
    def _(n):
        rows_of, lanes, quarter = place_of(listing[n])
        for end in (0, (SZ + 1) * 8 * FLAT):
            out_ref[n, end : end + 8 * FLAT, :] = jnp.full((8 * FLAT, 128), -1.0, F32)

        for z in range(SZ):
            plane = jnp.zeros((8, 128), F32)
            for g in range(4):
                block = estimate_ref[z, rows_of(g), lanes]
                turned = pltpu.roll(block, (BX * (g - quarter)) % 128, axis=1)
                plane = jnp.where(group == g, turned, plane)
            before = pltpu.roll(plane, 1, axis=0)
            after = pltpu.roll(plane, 7, axis=0)
            wrapped_before = jnp.where(group == 0, -1.0, pltpu.roll(before, BX, axis=1))
            wrapped_after = jnp.where(group == 3, -1.0, pltpu.roll(after, 128 - BX, axis=1))
            versions = (
                jnp.where(row == 0, wrapped_before, before),
                plane,
                jnp.where(row == 7, wrapped_after, after),
            )
            at = (z + 1) * 8 * FLAT
            for b, version in enumerate(versions):
                for c in range(-2, 3):
                    moved = version
                    if c != 0:
                        moved = pltpu.roll(version, -c % 128, axis=1)
                        inside = (column + c >= 0) & (column + c < BX)
                        moved = jnp.where(inside, moved, -1.0)
                    out_ref[n, pl.ds(at + 5 * b + c + 2, 8, stride=FLAT), :] = moved
            out_ref[n, pl.ds(at + 15, 8, stride=FLAT), :] = jnp.full((8, 128), -1.0, F32)


def bricks_kernel(
    tissue_ref, estimate_ref, moments_ref, stack_ref, w1_ref, w2_ref, w3_ref, b3_ref,
    out_ref, listing, hidden, partial, result,
):
    means = moments_ref[:, 0:1]
    centre = jnp.sum(means, axis=0, keepdims=True) / DEVICES
    deviation = jnp.sum(moments_ref[:, 1:2] + LOCAL * (means - centre) ** 2, axis=0, keepdims=True)
    spread = jnp.sqrt(deviation / COUNT + 1e-06)
    scale = 1.0 / spread
    out_ref[...] = estimate_ref[...]
    many = note_bricks(tissue_ref, listing)
    group = iota((8, 128), 1) // BX
    tall_group = iota((3 * CH, 128), 1) // BX

    fixed_row = iota((TALL - STACK, 128), 0)
    fixed_column = iota((TALL - STACK, 128), 1) % BX
    fixed = fixed_row < 2
    fixed |= (fixed_row == 2) & (fixed_column == 0)
    fixed |= (fixed_row == 3) & (fixed_column == BX - 1)
    fixed = jnp.where(fixed, 1.0, 0.0).astype(BF16)
    fixed = jnp.concatenate([fixed, fixed], axis=1)

    @pl.loop(0, many)
    def _(n):
        rows_of, lanes, quarter = place_of(listing[n])

        for z in range(SZ):
            for pair in range(4):
                taps = []
                for r in (2 * pair, 2 * pair + 1):
                    at = [((z + a) * 8 + r) * FLAT for a in range(3)]
                    taps.append(
                        jnp.concatenate([stack_ref[n, k : k + FLAT, :] for k in at], axis=0)
                    )
                taps = jnp.concatenate(taps, axis=1)
                taps = jnp.where(taps < 0.0, 0.0, (taps - centre) * scale).astype(BF16)
                taps = jnp.concatenate([taps, fixed], axis=0)
                first = jnp.dot(
                    w1_ref[...], taps, preferred_element_type=F32
                )
                first = jnp.maximum(first, 0.0)
                for e in range(2):
                    r = 2 * pair + e
                    value = first[:, 128 * e : 128 * (e + 1)]
                    hidden[z, r + 1] = value.astype(BF16)
                    if r == 7:
                        turned = pltpu.roll(value, BX, axis=1)
                        hidden[z, 0] = jnp.where(tall_group == 0, 0.0, turned).astype(BF16)
                    if r == 0:
                        turned = pltpu.roll(value, 128 - BX, axis=1)
                        hidden[z, 9] = jnp.where(tall_group == 3, 0.0, turned).astype(BF16)

        ones = jnp.ones((DEEP - 9 * CH, 256), BF16)
        last_weights = jnp.broadcast_to(w3_ref[...].astype(F32), (16, CH)).astype(BF16)
        for z in range(SZ):
            for pair in range(4):
                taps = [
                    hidden[z, 2 * pair + e : 2 * pair + e + 3].reshape(9 * CH, 128) for e in range(2)
                ]
                taps = jnp.concatenate([jnp.concatenate(taps, axis=1), ones], axis=0)
                partial[z, pair] = jnp.dot(w2_ref[...], taps, preferred_element_type=F32)

        for z in range(SZ):
            for pair in range(4):
                total = partial[z, pair, CH : 2 * CH]
                if z > 0:
                    total += partial[z - 1, pair, :CH]
                if z < SZ - 1:
                    total += partial[z + 1, pair, 2 * CH :]
                second = jnp.maximum(total, 0.0).astype(BF16)
                last = jnp.dot(last_weights, second, preferred_element_type=F32)
                result[z, 2 * pair : 2 * pair + 1, :] = last[0:1, :128]
                result[z, 2 * pair + 1 : 2 * pair + 2, :] = last[0:1, 128:]

        for z in range(SZ):
            change = (result[z] + b3_ref[0]) * spread
            for g in range(4):
                turned = pltpu.roll(change, (BX * (quarter - g)) % 128, axis=1)
                out_ref[z, rows_of(g), lanes] += jnp.where(group == quarter, turned, 0.0)


def body(observed, psf_taps, psf_index, tissue, w_first, b_first, w_mid, b_mid, w_last, b_last):
    slabs = NZ // SZ
    first_pairs = [(i, i ^ 1) for i in range(slabs)]
    second_pairs = [(i, ((((i + 1) % slabs) ^ 1) - 1) % slabs) for i in range(slabs)]
    swap = [(0, 1), (1, 0)]
    volume = shape((SZ, SY, NX), F32)
    planes = shape((R, SY, NX), BF16)

    def beside(first, second):
        return lax.ppermute(first, "gz", first_pairs), lax.ppermute(second, "gz", second_pairs)

    wide = shape((SZ, SY, WIDE), F32)
    first, second, edge = call(
        prepare_kernel, [planes, planes, shape((SZ, HALO, WIDE), F32)], [observed], [VMEM], limit=8
    )
    first, second = beside(first, second)
    observed_edge = lax.ppermute(edge, "gy", swap)

    table, rows_f, rows_a, cols_f, cols_a, shifted, picked_y, picked_x = call(
        setup_kernel,
        [
            shape((2 * SZ * ROWS, 128), F32),
            shape((SZ, EXT, 256), BF16),
            shape((SZ, SY, 256), BF16),
            shape((SZ, 256, 256), BF16),
            shape((SZ, 256, 256), BF16),
            wide,
            shape((128, 128), F32),
            shape((128, 128), F32),
        ],
        [psf_taps.transpose(1, 0, 2), psf_index, observed],
        [VMEM, SMEM, VMEM],
        scratch=[
            pltpu.VMEM((3 * MODELS, 128), F32),
            pltpu.VMEM((128, 128), F32),
            pltpu.VMEM((ROWS, 128), F32),
            pltpu.VMEM((ROWS, 128), F32),
        ],
        flops=100_000_000,
    )

    def own_planes(kind, volume_in):
        (out,) = call(
            functools.partial(own_planes_kernel, kind),
            [volume], [table, volume_in], [VMEM, VMEM], flops=16 * SZ * SY * NX,
        )
        return out

    estimate = observed
    for turn in range(2):
        u, u_edge = call(
            forward_planes_kernel,
            [volume, shape((SZ, HALO, NX), BF16)],
            [table, own_planes(0, estimate), first, second],
            [VMEM] * 4,
            flops=30 * SZ * SY * NX,
        )
        u_edge = lax.ppermute(u_edge, "gy", swap)
        q, first, second = call(
            ratio_kernel,
            [volume, planes, planes],
            [u, u_edge, shifted, observed_edge, rows_f, rows_a, cols_f, cols_a],
            [VMEM] * 8,
            scratch=[pltpu.VMEM((SZ, EXT, NX), F32), pltpu.VMEM((SZ, EXT, WIDE), F32)],
            flops=1_000_000_000,
            limit=24,
        )
        first, second = beside(first, second)
        if turn == 0:
            inverse, w1, w2 = call(
                second_setup_kernel,
                [volume, shape((3 * CH, TALL), BF16), shape((3 * CH, DEEP), BF16)],
                [
                    table, picked_y, picked_x, w_first, b_first[None], w_mid, b_mid[None], q,
                ],
                [VMEM] * 7 + [pl.BlockSpec(memory_space=pl.ANY)],
                scratch=[pltpu.VMEM((128, NX), F32)],
                flops=100_000_000,
            )
        ins = [table, own_planes(1, q), first, second, estimate, inverse]
        specs = [VMEM] * 6
        if turn == 0:
            estimate, first, second = call(
                update_kernel, [volume, planes, planes], ins, specs, flops=30 * SZ * SY * NX
            )
            first, second = beside(first, second)
        else:
            estimate, own_moments = call(
                last_update_kernel,
                [volume, shape((DEVICES, 128), F32)],
                ins,
                specs,
                flops=30 * SZ * SY * NX,
            )
    moments = lax.all_to_all(own_moments, ("gz", "gy"), 0, 0, tiled=True)

    (stack,) = call(
        stack_kernel,
        [shape((MOST, (SZ + 2) * 8 * FLAT, 128), F32)],
        [tissue, estimate],
        [SMEM, VMEM],
        scratch=[pltpu.SMEM((64,), jnp.int32)],
        flops=10_000_000,
    )
    (restored,) = call(
        bricks_kernel,
        [volume],
        [tissue, estimate, moments, stack, w1, w2, w_last[None], b_last],
        [SMEM] + [VMEM] * 6 + [SMEM],
        scratch=[
            pltpu.SMEM((64,), jnp.int32),
            pltpu.VMEM((SZ, 10, 3 * CH, 128), BF16),
            pltpu.VMEM((SZ, 4, 3 * CH, 256), F32),
            pltpu.VMEM((SZ, 8, 128), F32),
        ],
        flops=1_000_000_000,
        limit=24,
    )
    return restored


def solution(mesh):
    return jax.shard_map(
        body,
        mesh=mesh,
        in_specs=(P("gz", "gy", None), P(), P(), P("gz", "gy", None), P(), P(), P(), P(), P(), P()),
        out_specs=P("gz", "gy", None),
        check_vma=False,
    )
```
